512 devices in a mesh: node: 16 (over z), local: 8 (over x, core), dp: 4 (over y).
Axes of the slice: x: 4, y: 4, z: 16, core: 2. Of those that a mesh axis runs over, the one named last changes fastest.
Arguments:
- layer_input: bfloat16 [8192, 2560], P(('node', 'dp'), 'local'), may hold values from -6 to 6
- grad_out: bfloat16 [8192, 2560], P(('node', 'dp'), 'local'), may hold values from -6 to 6
- gate_values: bfloat16 [8192, 6], P(('node', 'dp')), may hold values from 0.049804688 to 0.5
- route_expert: int32 [8192, 6], P(('node', 'dp')), may hold values from 0 to 159, as said below
- route_slot: int32 [8192, 6], P(('node', 'dp')), may hold values from -1 to 5, as said below
- shared_gate: bfloat16 [1536, 2560], P('local', 'dp'), may hold values from -0.125 to 0.125
- shared_up: bfloat16 [1536, 2560], P('local', 'dp'), may hold values from -0.125 to 0.125
- shared_down: bfloat16 [1536, 2560], P('local', 'dp'), may hold values from -0.15625 to 0.15625
- expert_gate: bfloat16 [64, 768, 2560], P(('node', 'dp'), 'local'), may hold values from -0.125 to 0.125
- expert_up: bfloat16 [64, 768, 2560], P(('node', 'dp'), 'local'), may hold values from -0.125 to 0.125
- expert_down: bfloat16 [64, 768, 2560], P(('node', 'dp'), 'local'), may hold values from -0.21875 to 0.21875
Outputs:
- grad_x: bfloat16 [8192, 2560], P(('node', 'dp'), 'local')
- grad_gates: float32 [8192, 6], P(('node', 'dp'))
- grad_shared_gate: bfloat16 [1536, 2560], P('local', 'dp')
- grad_shared_up: bfloat16 [1536, 2560], P('local', 'dp')
- grad_shared_down: bfloat16 [1536, 2560], P('local', 'dp')
- grad_expert_gate: bfloat16 [64, 768, 2560], P(('node', 'dp'), 'local')
- grad_expert_up: bfloat16 [64, 768, 2560], P(('node', 'dp'), 'local')
- grad_expert_down: bfloat16 [64, 768, 2560], P(('node', 'dp'), 'local')
The draws below stay inside these ranges and needn't reach their ends.
Inputs may be any that keep to these rules, and one draw needn't show every extreme that they name: `route_expert`: each row names 6 different experts, all on at most 3 nodes; expert i lies on node i // 10. `route_slot`: for the choice of expert i, counting the choices of the 128 tokens of one group to the same expert in the order of rows, then of columns, from 0: the slot is that count, and it is -1 exactly where i % 10 >= 4 or the count reaches 6.
All inputs are finite; a program needn't handle non-finite values.
Results may differ from the reference program's by a relative error of at most 0.025.
Values may be sent and summed in bfloat16 or wider, within the bound.
A program may use at most 128 MiB of HBM per device.

```python
import jax
import jax.numpy as jnp
from jax import lax

D = 2560
FS = 1536
FR = 768
TOK = 128
TOPK = 6
NODE_LIMIT = 3
NODE_EXPERTS = 10
CAP = 6
EXPERTS = 64
TOKENS = 8192
N_NODE = 16
N_LOCAL = 8
N_DP = 4


def routing(key):
    groups = N_NODE * N_DP
    key_bias, key_node, key_hot, key_pick = jax.random.split(key, 4)
    node_bias = jax.random.randint(key_bias, (N_NODE,), 0, 2 ** 19)
    node_rand = jax.random.randint(key_node, (TOKENS, N_NODE), 0, 2 ** 20)
    hot_held = jax.random.randint(key_hot, (groups,), 0, N_NODE * N_DP)
    hot_node = hot_held // N_DP
    hot_id = hot_node * NODE_EXPERTS + hot_held % N_DP
    token_ids = jnp.arange(TOKENS, dtype=jnp.int32)
    group_ids = token_ids // TOK
    first_rows = token_ids % TOK < CAP
    node_ids = jnp.arange(N_NODE, dtype=jnp.int32)
    force_node = first_rows[:, None] & (node_ids[None, :] == hot_node[group_ids][:, None])
    node_score = (node_rand + node_bias[None, :] + force_node.astype(jnp.int32) * 2 ** 22) * N_NODE + node_ids[None, :]
    chosen = jnp.argsort(-node_score, axis=1, stable=True)[:, :NODE_LIMIT]
    width = NODE_LIMIT * NODE_EXPERTS
    candidates = (chosen[:, :, None] * NODE_EXPERTS + jnp.arange(NODE_EXPERTS, dtype=jnp.int32)[None, None, :]).reshape(TOKENS, width)
    pick_rand = jax.random.randint(key_pick, (TOKENS, width), 0, 2 ** 20)
    force_pick = first_rows[:, None] & (candidates == hot_id[group_ids][:, None])
    pick_score = (pick_rand + force_pick.astype(jnp.int32) * 2 ** 22) * width + jnp.arange(width, dtype=jnp.int32)[None, :]
    order = jnp.argsort(-pick_score, axis=1, stable=True)[:, :TOPK]
    expert_ids = jnp.take_along_axis(candidates, order, axis=1).astype(jnp.int32)
    inner = expert_ids % NODE_EXPERTS
    in_window = inner < N_DP
    held = expert_ids // NODE_EXPERTS * N_DP + inner
    onehot = ((held[:, :, None] == jnp.arange(N_NODE * N_DP, dtype=jnp.int32)[None, None, :]) & in_window[:, :, None]).astype(jnp.int32)
    onehot = onehot.reshape(groups, TOK * TOPK, N_NODE * N_DP)
    counts = jnp.cumsum(onehot, axis=1) - onehot
    ranks = jnp.sum(counts * onehot, axis=2).reshape(TOKENS, TOPK)
    slots = jnp.where(in_window & (ranks < CAP), ranks, -1).astype(jnp.int32)
    return (expert_ids, slots)


def draw_route_expert(key, part):
    expert_ids, slots = routing(key)
    return expert_ids


def draw_route_slot(key, part):
    expert_ids, slots = routing(key)
    return slots


def block_scale(stream_key, dims, cuts, low, high):
    gain, own = 1.0, jax.random.fold_in(stream_key, 6)
    for dim, blocks in cuts:
        draws = jnp.exp(jax.random.uniform(jax.random.fold_in(own, dim), (blocks,), jnp.float32, low / len(cuts), high / len(cuts)))
        gain = gain * jnp.repeat(draws, dims[dim] // blocks).reshape([-1 if axis == dim else 1 for axis in range(len(dims))])
    return gain


def centred(stream_key, shape, scale, reach, cuts=(), held_as=jnp.bfloat16):
    factor_of = block_scale(stream_key, shape, cuts, -0.22, 0.18) if cuts else 1.0
    entries = jax.random.normal(stream_key, shape, jnp.float32) * scale * factor_of
    return jnp.minimum(jnp.maximum(entries, -reach), reach).astype(held_as)


def setup_inputs(seed: int = 0) -> dict:
    key_of = jax.random.split(jax.random.key(seed), 12)
    layer_input = centred(key_of[0], (TOKENS, D), 1.0, 6.0, ((0, 64), (1, 8)))
    grad_out = centred(key_of[1], (TOKENS, D), 1.0, 6.0, ((0, 64), (1, 8)))
    gate_values = jnp.clip(0.049804688 + 0.4501953 * jax.random.uniform(key_of[2], (TOKENS, TOPK), jnp.float32) ** block_scale(key_of[2], (TOKENS, TOPK), ((0, 64),), -0.2, 0.2), 0.049804688, 0.5).astype(jnp.bfloat16)
    route_expert = draw_route_expert(jax.random.fold_in(key_of[11], 71), 0)
    route_slot = draw_route_slot(jax.random.fold_in(key_of[11], 71), 0)
    shared_gate = centred(key_of[5], (FS, D), D ** -0.5, 0.125, ((0, 8), (1, 4)))
    shared_up = centred(key_of[6], (FS, D), D ** -0.5, 0.125, ((0, 8), (1, 4)))
    shared_down = centred(key_of[7], (FS, D), FS ** -0.5, 0.15625, ((0, 8), (1, 4)))
    expert_gate = centred(key_of[8], (EXPERTS, FR, D), D ** -0.5, 0.125, ((0, 64), (1, 8)))
    expert_up = centred(key_of[9], (EXPERTS, FR, D), D ** -0.5, 0.125, ((0, 64), (1, 8)))
    expert_down = centred(key_of[10], (EXPERTS, FR, D), FR ** -0.5, 0.21875, ((0, 64), (1, 8)))
    return {"layer_input": layer_input, "grad_out": grad_out, "gate_values": gate_values, "route_expert": route_expert, "route_slot": route_slot, "shared_gate": shared_gate, "shared_up": shared_up, "shared_down": shared_down, "expert_gate": expert_gate, "expert_up": expert_up, "expert_down": expert_down}


def reference(layer_input, grad_out, gate_values, route_expert, route_slot, shared_gate, shared_up, shared_down, expert_gate, expert_up, expert_down):
    groups = N_NODE * N_DP
    shared_a = jnp.dot(layer_input, shared_gate.T, preferred_element_type=jnp.float32)
    shared_b = jnp.dot(layer_input, shared_up.T, preferred_element_type=jnp.float32)
    sigm_a = jax.nn.sigmoid(shared_a)
    silu_a = shared_a * sigm_a
    shared_h = (silu_a * shared_b).astype(jnp.bfloat16)
    shared_e = jnp.dot(grad_out, shared_down.T, preferred_element_type=jnp.float32)
    shared_da = (shared_e * shared_b * sigm_a * (1.0 + shared_a * (1.0 - sigm_a))).astype(jnp.bfloat16)
    shared_db = (shared_e * silu_a).astype(jnp.bfloat16)

    slice_width = FS // N_LOCAL
    shared_dx = jnp.zeros((TOKENS, D), jnp.float32)
    for piece in range(N_LOCAL):
        lower = piece * slice_width
        upper = lower + slice_width
        term = jnp.dot(shared_da[:, lower:upper], shared_gate[lower:upper, :], preferred_element_type=jnp.float32)
        term = term + jnp.dot(shared_db[:, lower:upper], shared_up[lower:upper, :], preferred_element_type=jnp.float32)
        shared_dx = shared_dx + term.astype(jnp.bfloat16).astype(jnp.float32)

    def group_step(carry, items):
        x_group, dy_group, da_group, db_group, h_group = items
        part_gate = jnp.dot(da_group.T, x_group, preferred_element_type=jnp.float32)
        part_up = jnp.dot(db_group.T, x_group, preferred_element_type=jnp.float32)
        part_down = jnp.dot(h_group.T, dy_group, preferred_element_type=jnp.float32)
        carry = (carry[0] + part_gate.astype(jnp.bfloat16).astype(jnp.float32),
                 carry[1] + part_up.astype(jnp.bfloat16).astype(jnp.float32),
                 carry[2] + part_down.astype(jnp.bfloat16).astype(jnp.float32))
        return carry, None

    start_sums = (jnp.zeros((FS, D), jnp.float32), jnp.zeros((FS, D), jnp.float32), jnp.zeros((FS, D), jnp.float32))
    items = (layer_input.reshape(groups, TOK, D), grad_out.reshape(groups, TOK, D), shared_da.reshape(groups, TOK, FS),
             shared_db.reshape(groups, TOK, FS), shared_h.reshape(groups, TOK, FS))
    sums, unused = lax.scan(group_step, start_sums, items)
    grad_shared_gate = sums[0].astype(jnp.bfloat16)
    grad_shared_up = sums[1].astype(jnp.bfloat16)
    grad_shared_down = sums[2].astype(jnp.bfloat16)

    block_rows = groups * CAP
    kept = route_slot >= 0
    held = (route_expert // NODE_EXPERTS) * N_DP + route_expert % NODE_EXPERTS
    token_ids = jnp.arange(TOKENS, dtype=jnp.int32)
    group_ids = (token_ids // TOK)[:, None]
    position = held * block_rows + group_ids * CAP + route_slot
    position = jnp.where(kept, position, EXPERTS * block_rows).astype(jnp.int32)
    flat_ids = jnp.arange(TOKENS * TOPK, dtype=jnp.int32)
    table = jnp.full((EXPERTS * block_rows,), TOKENS * TOPK, jnp.int32)
    table = table.at[position.reshape(-1)].set(flat_ids, mode="drop").reshape(EXPERTS, block_rows)

    x_padded = jnp.concatenate([layer_input, jnp.zeros((1, D), layer_input.dtype)], axis=0)
    dy_padded = jnp.concatenate([grad_out, jnp.zeros((1, D), grad_out.dtype)], axis=0)
    gate_padded = jnp.concatenate([gate_values.reshape(-1), jnp.zeros((1,), gate_values.dtype)], axis=0)

    def expert_step(carry, items):
        dx_total, gate_total = carry
        choice_ids, weight_gate, weight_up, weight_down = items
        token_rows = choice_ids // TOPK
        rows_x = x_padded[token_rows]
        rows_dy = dy_padded[token_rows]
        weight_q = gate_padded[choice_ids].astype(jnp.float32)[:, None]
        pre_a = jnp.dot(rows_x, weight_gate.T, preferred_element_type=jnp.float32)
        pre_b = jnp.dot(rows_x, weight_up.T, preferred_element_type=jnp.float32)
        back_e = jnp.dot(rows_dy, weight_down.T, preferred_element_type=jnp.float32)
        sigm_b = jax.nn.sigmoid(pre_a)
        silu_b = pre_a * sigm_b
        hidden = silu_b * pre_b
        gate_grad = jnp.sum(back_e * hidden, axis=1)
        grad_a = (weight_q * back_e * pre_b * sigm_b * (1.0 + pre_a * (1.0 - sigm_b))).astype(jnp.bfloat16)
        grad_b = (weight_q * back_e * silu_b).astype(jnp.bfloat16)
        hidden_q = (weight_q * hidden).astype(jnp.bfloat16)
        new_gate = jnp.dot(grad_a.T, rows_x, preferred_element_type=jnp.float32).astype(jnp.bfloat16)
        new_up = jnp.dot(grad_b.T, rows_x, preferred_element_type=jnp.float32).astype(jnp.bfloat16)
        new_down = jnp.dot(hidden_q.T, rows_dy, preferred_element_type=jnp.float32).astype(jnp.bfloat16)
        row_dx = jnp.dot(grad_a, weight_gate, preferred_element_type=jnp.float32)
        row_dx = row_dx + jnp.dot(grad_b, weight_up, preferred_element_type=jnp.float32)
        dx_total = dx_total.at[token_rows].add(row_dx)
        gate_total = gate_total.at[choice_ids].set(gate_grad)
        return (dx_total, gate_total), (new_gate, new_up, new_down)

    start_carry = (jnp.zeros((TOKENS + 1, D), jnp.float32), jnp.zeros((TOKENS * TOPK + 1,), jnp.float32))
    carry, weights_out = lax.scan(expert_step, start_carry, (table, expert_gate, expert_up, expert_down))
    routed_dx = carry[0][:TOKENS]
    grad_gates = carry[1][:TOKENS * TOPK].reshape(TOKENS, TOPK)
    grad_x = (shared_dx + routed_dx).astype(jnp.bfloat16)
    return (grad_x, grad_gates, grad_shared_gate, grad_shared_up, grad_shared_down,
            weights_out[0], weights_out[1], weights_out[2])
```

```python
import jax
import jax.numpy as jnp
from jax import lax
from jax.experimental import pallas as pl
from jax.experimental.pallas import tpu as pltpu
from jax.sharding import PartitionSpec as P

BF = jnp.bfloat16
F32 = jnp.float32
MESH = pl.DeviceIdType.MESH


def nt(a, b):
    return lax.dot_general(a, b, (((1,), (1,)), ((), ())), preferred_element_type=F32)


def nn(a, b):
    return lax.dot_general(a, b, (((1,), (0,)), ((), ())), preferred_element_type=F32)


def tn(a, b):
    return lax.dot_general(a, b, (((0,), (0,)), ((), ())), preferred_element_type=F32)


def iota(shape, dim):
    return lax.broadcasted_iota(jnp.int32, shape, dim)


def sixth(v):
    return lax.shift_right_arithmetic(v * 43, 8)


def one(mask):
    return jnp.where(mask, 1.0, 0.0).astype(BF)


def take(ref, sem):
    pltpu.make_async_copy(ref, ref, sem).wait()


def kernel(
    x_ref, dy_ref, gv_ref, re_ref, rs_ref, sg_ref, su_ref, sd_ref, eg_ref, eu_ref, ed_ref,
    gx_ref, gg_ref, gsg_ref, gsu_ref, gsd_ref, neg_ref, neu_ref, ned_ref,
    tx, pb, pr, vcat, qm, qr, rall, qv, xf, df, wgu, dab, hq, pkb, s1, s2, s3, ret, back, rd,
    xs, xa, da, wsg, sp, r2, sdall, dxp, dxs, dxf, dxr, gp, arr, arl, fo,
    tok_send, tok_recv, tsib_send, tsib_recv, disp_send, disp_recv,
    ag_send, ag_recv, as_send, as_recv, y_send, y_recv, y2_send, y2_recv,
    ds_send, ds_recv, dx_send, dx_recv, rr_send, rr_recv, rl_send, rl_recv,
    br_send, br_recv, bl_send, bl_recv, c_send, c_recv, r_send, r_recv, b_send, b_recv,
):
    z = lax.axis_index("node")
    y = lax.axis_index("dp")
    l = lax.axis_index("local")
    x = l // 2
    c = l % 2
    oc = 1 - c

    def loc(xx, cc):
        return xx * 2 + cc

    bar = pltpu.get_barrier_semaphore()

    def greet(zz, ll, yy):
        pl.semaphore_signal(bar, inc=1, device_id=(zz, ll, yy), device_id_type=MESH)

    greet(z, loc(x, oc), y)

    def greet_plane(i, _):
        p = (x * 4 + y + 1 + i) % 16
        greet(z, loc(p // 4, c), p % 4)
        return 0

    lax.fori_loop(0, 15, greet_plane, 0)

    def greet_z(i, _):
        greet((z + 1 + i // 4) % 16, l, i % 4)
        return 0

    lax.fori_loop(0, 60, greet_z, 0)

    xv = x_ref[...].astype(F32)
    dv = dy_ref[...].astype(F32)
    even = jnp.concatenate([xv, dv[:, 256:320], dv[:, :256]], axis=1)
    odd = jnp.concatenate([xv[:, 64:320], dv[:, 0:64], xv[:, 0:64], dv[:, 64:320]], axis=1)
    is_even = c == 0
    tx[...] = jnp.where(is_even, even, odd).astype(BF)

    re = re_ref[...]
    rs = rs_ref[...]
    nd = lax.shift_right_arithmetic(re * 205, 11)
    ex = jnp.where(rs >= 0, lax.rem(nd + 16 - z, 16) * 4 + (re - nd * 10), -1)
    lane = iota((128, 128), 1)
    both = jnp.zeros((128, 128), F32)
    exf = ex.astype(F32)
    rsf = rs.astype(F32)
    gvf = gv_ref[...].astype(F32)
    for k in range(6):
        both = jnp.where(lane == k, exf[:, k : k + 1], both)
        both = jnp.where(lane == 8 + k, rsf[:, k : k + 1], both)
        vcat[k * 128 : (k + 1) * 128, :] = jnp.where(
            lane == rs[:, k : k + 1], gvf[:, k : k + 1], 0.0
        ).astype(BF)
    both_t = both.T
    e_t = both_t[0:8, :].astype(jnp.int32)
    s_t = both_t[8:16, :].astype(jnp.int32)
    p_t = jnp.where(e_t >= 0, e_t * 6 + s_t, -1)

    pl.semaphore_wait(bar, 76)

    for i in range(4):
        own = jnp.logical_and(x == i, y == x)

        @pl.when(own)
        def _():
            pltpu.make_async_copy(tx, xs.at[y, c], tok_recv.at[y]).start()

        @pl.when(jnp.logical_not(own))
        def _():
            pltpu.make_async_remote_copy(
                tx, xs.at[y, c], tok_send.at[i], tok_recv.at[y],
                device_id=(z, loc(i, c), x), device_id_type=MESH,
            ).start()

    row = iota((128, 128), 0)
    ry = lax.shift_right_arithmetic(row, 5)
    rr = row & 31
    rt = sixth(rr)
    rc = rr - rt * 6

    def chunk(i, _):
        k = i // 2
        h = i % 2
        dz = (8 - k) * (1 - h) + (8 + k) * ((k + 7) // 8) * h
        code = jnp.where(rr < 30, (dz * 4 + ry) * 6 + rc, -7)
        ecode = jnp.where(rr == 30, dz * 4 + ry, -7)
        hit = code == p_t[0:1, :]
        for kk in range(1, 6):
            hit = jnp.logical_or(hit, code == p_t[kk : kk + 1, :])
        prod = nn(one(hit), tx[...])
        out = nn(
            jnp.concatenate([one(ecode == e_t[kk : kk + 1, :]) for kk in range(6)], axis=1), vcat[...]
        )
        for t in range(5):
            out = out + jnp.where(rt == t, prod[:, t * 128 : (t + 1) * 128], 0.0)
        pb[dz] = out.astype(BF).reshape(4, 32, 128)
        for j in range(4):
            own = jnp.logical_and(dz == 0, y == j)

            @pl.when(own)
            def _():
                pltpu.make_async_copy(pb.at[dz, j], pr.at[dz, y], disp_recv.at[k]).start()

            @pl.when(jnp.logical_not(own))
            def _():
                pltpu.make_async_remote_copy(
                    pb.at[dz, j], pr.at[dz, y], disp_send, disp_recv.at[k],
                    device_id=((z + dz) % 16, l, j), device_id_type=MESH,
                ).start()
        return 0

    lax.fori_loop(0, 16, chunk, 0)

    col = iota((288, 256), 1)
    qrow = iota((288, 256), 0)
    cr = col & 31
    ct = sixth(cr)
    cb = lax.shift_right_arithmetic(col, 5) * 6
    dest = ct * 48 + cb + (cr - ct * 6)
    gate_row = qrow - 240 - cb
    qm[...] = one(
        jnp.logical_or(
            jnp.logical_and(cr < 30, qrow == dest),
            jnp.logical_and(cr == 30, jnp.logical_and(gate_row >= 0, gate_row < 6)),
        )
    )
    orow = iota((128, 240), 0)
    ocol = iota((128, 240), 1)
    og = lax.shift_right_arithmetic(orow, 4) * 6
    orr = orow & 15
    keep = jnp.logical_and(orr < 6, ocol == og + orr)
    keep = jnp.logical_or(keep, jnp.logical_and(jnp.logical_and(orr >= 6, orr < 12), ocol == 48 + og + orr - 6))
    tail = jnp.logical_and(orr >= 12, orr < 15)
    keep = jnp.logical_or(keep, jnp.logical_and(tail, ocol == 96 + og + orr - 12))
    keep = jnp.logical_or(keep, jnp.logical_and(tail, ocol == 144 + og + orr - 9))
    goff = ocol - 192 - og
    keep = jnp.logical_or(keep, jnp.logical_and(orr == 15, jnp.logical_and(goff >= 0, goff < 6)))
    qr[...] = one(keep)
    wgu[0:96, :] = eg_ref[0]
    wgu[96:192, :] = eu_ref[0]
    wsg[0:192, :] = sg_ref[...]
    wsg[192:384, :] = su_ref[...]

    lane48 = iota((48, 128), 1)
    row48 = iota((48, 128), 0)
    low48 = lane48 < 64
    c48 = row48 - sixth(row48) * 6

    for i in range(4):
        take(xs.at[i, c], tok_recv.at[i])
        pltpu.make_async_remote_copy(
            xs.at[i, c], xs.at[i, c], tsib_send.at[i], tsib_recv.at[i],
            device_id=(z, loc(x, oc), y), device_id_type=MESH,
        ).start()
    low128 = lane < 64
    for i in range(4):
        take(xs.at[i, oc], tsib_recv.at[i])
        te = xs[i, 0]
        to = xs[i, 1]
        te_t = te[:, 256:384].astype(F32)
        to_t = to[:, 256:384].astype(F32)
        rows = pl.ds(i * 128, 128)
        xa[rows, 0:256] = te[:, 0:256]
        xa[rows, 256:384] = jnp.where(low128, te_t, to_t).astype(BF)
        xa[rows, 384:640] = to[:, 0:256]
        da[rows, 0:256] = te[:, 384:640]
        da[rows, 256:384] = jnp.where(low128, pltpu.roll(te_t, 64, 1), pltpu.roll(to_t, 64, 1)).astype(BF)
        da[rows, 384:640] = to[:, 384:640]
    for i in range(4):
        rows = pl.ds(i * 128, 128)
        sp[i, :, 0:384] = nt(xa[rows, :], wsg[...]).astype(BF)
        sp[i, :, 384:576] = nt(da[rows, :], sd_ref[...]).astype(BF)
        sp[i, :, 576:640] = jnp.zeros((128, 64), BF)
    for o in range(1, 4):
        to_y = (y + o) % 4
        pltpu.make_async_remote_copy(
            sp.at[to_y], r2.at[y], y_send.at[o], y_recv.at[o],
            device_id=(z, l, to_y), device_id_type=MESH,
        ).start()
    r2[y] = sp[y]
    for o in range(1, 4):
        take(r2.at[(y + 4 - o) % 4], y_recv.at[o])
    tot = r2[0].astype(F32) + r2[1].astype(F32) + r2[2].astype(F32) + r2[3].astype(F32)
    sa = tot[:, 0:192]
    sb = tot[:, 192:384]
    se = tot[:, 384:576]
    sig = 1.0 / (1.0 + jnp.exp(-sa))
    sil = sa * sig
    sdall[y] = jnp.concatenate(
        [
            se * sb * sig * (1.0 + sa * (1.0 - sig)),
            se * sil,
            sil * sb,
            jnp.zeros((128, 64), F32),
        ],
        axis=1,
    ).astype(BF)
    for o in range(1, 4):
        pltpu.make_async_remote_copy(
            sdall.at[y], sdall.at[y], y2_send.at[o], y2_recv.at[o],
            device_id=(z, l, (y + o) % 4), device_id_type=MESH,
        ).start()
    for o in range(1, 4):
        take(sdall.at[(y + 4 - o) % 4], y2_recv.at[o])
    sall = sdall[...].reshape(512, 640)
    for t in range(5):
        cols = slice(t * 128, (t + 1) * 128)
        g2 = tn(sall[:, 0:384], xa[:, cols])
        g1 = tn(sall[:, 384:640], da[:, cols])
        gp[t * 3] = g2[0:192].astype(BF)
        gp[t * 3 + 1] = g2[192:384].astype(BF)
        gp[t * 3 + 2] = g1[0:192].astype(BF)
    gp[15] = jnp.zeros((192, 128), BF)

    zr = (z + 1) % 16
    zl = (z + 15) % 16

    def send_right(src, dst, ss, rsem):
        pltpu.make_async_remote_copy(
            src, dst, ss, rsem, device_id=(zr, l, y), device_id_type=MESH
        ).start()

    def send_left(src, dst, ss, rsem):
        pltpu.make_async_remote_copy(
            src, dst, ss, rsem, device_id=(zl, l, y), device_id_type=MESH
        ).start()

    def ring_sum(s):
        if s == 1:
            send_right(gp.at[(z + 8) % 16], arr.at[0], rr_send.at[0], rr_recv.at[0])
            send_left(gp.at[(z + 9) % 16], arl.at[0], rl_send.at[0], rl_recv.at[0])
            return
        if s <= 8:
            q = s - 2
            take(arr.at[q], rr_recv.at[q])
            arr[q] = (arr[q].astype(F32) + gp[(z + 9 - s) % 16].astype(F32)).astype(BF)
            send_right(arr.at[q], arr.at[q + 1], rr_send.at[q + 1], rr_recv.at[q + 1])
            if s <= 7:
                take(arl.at[q], rl_recv.at[q])
                arl[q] = (arl[q].astype(F32) + gp[(z + 8 + s) % 16].astype(F32)).astype(BF)
                send_left(arl.at[q], arl.at[q + 1], rl_send.at[q + 1], rl_recv.at[q + 1])
            return
        if s == 9:
            take(arr.at[7], rr_recv.at[7])
            take(arl.at[6], rl_recv.at[6])
            fo[z] = (gp[z].astype(F32) + arr[7].astype(F32) + arl[6].astype(F32)).astype(BF)
        q = s - 9
        if q > 0 and q <= 8:
            take(fo.at[(z + 16 - q) % 16], br_recv.at[q - 1])
        if q > 0 and q <= 7:
            take(fo.at[(z + q) % 16], bl_recv.at[q - 1])
        if q < 8:
            src = fo.at[(z + 16 - q) % 16]
            send_right(src, src, br_send.at[q], br_recv.at[q])
        if q < 7:
            src = fo.at[(z + q) % 16]
            send_left(src, src, bl_send.at[q], bl_recv.at[q])

    ring_sum(1)

    for i in range(4):
        part = nn(sall[i * 128 : (i + 1) * 128, 0:384], wsg[...]).astype(BF)
        dxp[0, i] = part[:, 0:384]
        dxp[1, i] = part[:, 256:640]
    dx_sib = pltpu.make_async_remote_copy(
        dxp.at[oc], dxs, ds_send, ds_recv, device_id=(z, loc(x, oc), y), device_id_type=MESH
    )
    dx_sib.start()

    ring_sum(2)

    def unpack(k):
        a = 8 - k
        b = (8 + k) % 16 if k else 0
        take(pr.at[0:2], disp_recv.at[k])
        u = nn(qm[...], jnp.concatenate([pr[a].reshape(128, 128), pr[b].reshape(128, 128)], axis=0))
        for t in range(5):
            rall[x, c, k, :, t * 128 : (t + 1) * 128] = u[t * 48 : (t + 1) * 48].astype(BF)
        q = jnp.sum(jnp.where(lane48 == c48, u[240:288], 0.0), axis=1, keepdims=True)
        qv[k * 48 : (k + 1) * 48, :] = jnp.broadcast_to(q, (48, 128))
        blk = rall.at[x, c, k]
        for n, dx in enumerate((1, 3)):
            pltpu.make_async_remote_copy(
                blk, blk, ag_send.at[k, n], ag_recv.at[k, n],
                device_id=(z, loc((x + dx) % 4, c), y), device_id_type=MESH,
            ).start()
        pltpu.make_async_remote_copy(
            blk, blk, as_send.at[k, 0], as_recv.at[k, 0],
            device_id=(z, loc(x, oc), y), device_id_type=MESH,
        ).start()

    def to_sib(blk, k, n):
        pltpu.make_async_remote_copy(
            blk, blk, as_send.at[k, n], as_recv.at[k, n],
            device_id=(z, loc(x, oc), y), device_id_type=MESH,
        ).start()

    def forward(k):
        left = rall.at[(x + 3) % 4, c, k]
        right = rall.at[(x + 1) % 4, c, k]
        take(left, ag_recv.at[k, 0])
        if k % 2 == 0:
            pltpu.make_async_remote_copy(
                left, left, ag_send.at[k, 2], ag_recv.at[k, 2],
                device_id=(z, loc((x + 1) % 4, c), y), device_id_type=MESH,
            ).start()
        to_sib(left, k, 1)
        take(right, ag_recv.at[k, 1])
        if k % 2 == 1:
            pltpu.make_async_remote_copy(
                right, right, ag_send.at[k, 2], ag_recv.at[k, 2],
                device_id=(z, loc((x + 3) % 4, c), y), device_id_type=MESH,
            ).start()
        to_sib(right, k, 2)

    def across(k):
        far = rall.at[(x + 2) % 4, c, k]
        take(far, ag_recv.at[k, 2])
        to_sib(far, k, 3)

    def settle(k):
        for n, dx in enumerate((0, 3, 1, 2)):
            take(rall.at[(x + dx) % 4, oc, k], as_recv.at[k, n])

    def half(h):
        lo = 192 * h
        rows = slice(lo, lo + 192)
        lane192 = iota((192, 128), 1) < 64
        for p in range(4):
            te = rall[p, 0, 4 * h : 4 * h + 4].reshape(192, 640)
            to = rall[p, 1, 4 * h : 4 * h + 4].reshape(192, 640)
            te_t = te[:, 256:384].astype(F32)
            to_t = to[:, 256:384].astype(F32)
            b = p * 640
            xf[rows, b : b + 256] = te[:, 0:256]
            xf[rows, b + 256 : b + 384] = jnp.where(lane192, te_t, to_t).astype(BF)
            xf[rows, b + 384 : b + 640] = to[:, 0:256]
            df[rows, b : b + 256] = te[:, 384:640]
            df[rows, b + 256 : b + 384] = jnp.where(
                lane192, pltpu.roll(te_t, 64, 1), pltpu.roll(to_t, 64, 1)
            ).astype(BF)
            df[rows, b + 384 : b + 640] = to[:, 384:640]
        ab = nt(xf[rows, :], wgu[...])
        e = nt(df[rows, :], ed_ref[0])
        a = ab[:, 0:96]
        b = ab[:, 96:192]
        sg = 1.0 / (1.0 + jnp.exp(-a))
        sl = a * sg
        hid = sl * b
        gpart = jnp.sum(e * hid, axis=1, keepdims=True)
        q = qv[rows, 0:1]
        qe = q * e
        dab[rows, :] = jnp.concatenate([qe * b * sg * (1.0 + a * (1.0 - sg)), qe * sl], axis=1).astype(BF)
        hq[rows, :] = (q * hid).astype(BF)
        rd[...] = nn(dab[rows, :], wgu[...]).astype(BF)
        for k in range(4):
            r48 = slice(k * 48, (k + 1) * 48)
            g = jnp.where(lane48 == c48, gpart[r48], 0.0).astype(BF)
            zero = jnp.zeros((48, 128), F32)
            cols = []
            for p in range(4):
                t = rd[r48, p * 640 + 256 : p * 640 + 384].astype(F32)
                u = pltpu.roll(t, 64, 1)
                for cc in range(2):
                    b = p * 640 + cc * 384
                    first, second = (t, u) if cc == 0 else (u, t)
                    cols.append(
                        jnp.concatenate(
                            [
                                rd[r48, b : b + 128],
                                rd[r48, b + 128 : b + 256],
                                jnp.where(low48, first, zero).astype(BF),
                                jnp.where(low48, zero, second).astype(BF),
                                g,
                            ],
                            axis=0,
                        )
                    )
            packed = nn(qr[...], jnp.concatenate(cols, axis=1)).astype(BF)
            for ll in range(8):
                pkb[h, ll, k] = packed[:, ll * 128 : (ll + 1) * 128]
        for o in (2, 1, 3, 0):
            xx = (x + o) % 4
            pltpu.make_async_remote_copy(
                pkb.at[h, loc(xx, oc)], s1.at[h, xx], c_send.at[h, o], c_recv.at[h, o],
                device_id=(z, loc(x, oc), y), device_id_type=MESH,
            ).start()

    def reduce_pair(h):
        for o in (2, 1, 3, 0):
            xx = (x + o) % 4
            take(s1.at[h, xx], c_recv.at[h, o])
            v = (pkb[h, loc(xx, c)].astype(F32) + s1[h, xx].astype(F32)).astype(BF)
            if o == 0:
                s3[h, x] = v
            else:
                s2[h, xx] = v
                pltpu.make_async_remote_copy(
                    s2.at[h, xx], s3.at[h, x], r_send.at[h, o], r_recv.at[h, o],
                    device_id=(z, loc(xx, c), y), device_id_type=MESH,
                ).start()

    def give_back(h):
        for o in (1, 2, 3):
            take(s3.at[h, (x + 4 - o) % 4], r_recv.at[h, o])
        for k in range(4):
            v = s3[h, 0, k].astype(F32) + s3[h, 1, k].astype(F32)
            v = v + s3[h, 2, k].astype(F32) + s3[h, 3, k].astype(F32)
            ret[h, k] = v.astype(BF).reshape(8, 16, 128)
            kk = 4 * h + k
            for n, dz in enumerate((8 - kk, (8 + kk) % 16 if kk else 0)):
                for j in range(4):
                    src = ret.at[h, k, n * 4 + j]
                    dst = back.at[dz, y]
                    if dz == 0:

                        @pl.when(y == j)
                        def _():
                            pltpu.make_async_copy(src, dst, b_recv).start()

                        @pl.when(y != j)
                        def _():
                            pltpu.make_async_remote_copy(
                                src, dst, b_send, b_recv, device_id=(z, l, j), device_id_type=MESH
                            ).start()

                    else:
                        pltpu.make_async_remote_copy(
                            src, dst, b_send, b_recv,
                            device_id=((z + 16 - dz) % 16, l, j), device_id_type=MESH,
                        ).start()

    def dx_out():
        dx_sib.wait_recv()
        for i in range(4):
            own = jnp.logical_and(x == y, y == i)
            dxf[i] = (dxp[c, i].astype(F32) + dxs[i].astype(F32)).astype(BF)

            @pl.when(own)
            def _():
                pltpu.make_async_copy(dxf.at[i], dxr.at[x], dx_recv.at[x]).start()

            @pl.when(jnp.logical_not(own))
            def _():
                pltpu.make_async_remote_copy(
                    dxf.at[i], dxr.at[x], dx_send.at[i], dx_recv.at[x],
                    device_id=(z, loc(y, c), i), device_id_type=MESH,
                ).start()

    for k in range(4):
        unpack(k)
        if k >= 1:
            forward(k - 1)
        if k >= 2:
            across(k - 2)
    ring_sum(3)
    for k in range(4, 8):
        unpack(k)
        forward(k - 1)
        across(k - 2)
        if k % 2:
            ring_sum(4 + (k - 5) // 2)
    for k in range(4):
        settle(k)
    half(0)
    ring_sum(6)
    forward(7)
    across(6)
    reduce_pair(0)
    across(7)
    ring_sum(7)
    for k in range(4, 8):
        settle(k)
    half(1)
    ring_sum(8)
    give_back(0)
    reduce_pair(1)
    ring_sum(9)
    dx_out()
    ring_sum(10)
    give_back(1)

    def weight_grads(i, _):
        cols = pl.ds(pl.multiple_of(i * 640, 128), 640)
        g2 = tn(dab[...], xf[:, cols])
        neg_ref[0, :, cols] = g2[0:96].astype(BF)
        neu_ref[0, :, cols] = g2[96:192].astype(BF)
        ned_ref[0, :, cols] = tn(hq[...], df[:, cols]).astype(BF)
        return 0

    lax.fori_loop(0, 2, weight_grads, 0)
    ring_sum(11)
    lax.fori_loop(2, 4, weight_grads, 0)
    ring_sum(12)

    jc = iota((128, 1024), 1)
    jr = jc & 15
    jg = lax.shift_right_arithmetic(jc, 4) * 6
    cls_a = jr < 6
    cls_b = jnp.logical_and(jr >= 6, jr < 12)
    cls_t = jnp.logical_and(jr >= 12, jr < 15)
    code = jg + jnp.where(cls_a, jr, jnp.where(cls_b, jr - 6, jr - 12))
    pos = jnp.where(rs >= 0, ex * 6 + rs, -100)
    hit = code == pos[:, 0:1]
    hit2 = code + 3 == pos[:, 0:1]
    for kk in range(1, 6):
        hit = jnp.logical_or(hit, code == pos[:, kk : kk + 1])
        hit2 = jnp.logical_or(hit2, code + 3 == pos[:, kk : kk + 1])
    sel = jnp.concatenate(
        [
            one(jnp.logical_and(hit, cls_a)),
            one(jnp.logical_and(hit, cls_b)),
            one(jnp.logical_and(hit, cls_t)),
            one(jnp.logical_and(hit2, cls_t)),
        ],
        axis=0,
    )
    grow = one(jnp.logical_and(iota((64, 1024), 1) == iota((64, 1024), 0) * 16 + 15, True))
    ring_sum(13)

    take(back, b_recv)
    rows = back[...].reshape(1024, 128)
    got = nn(sel, rows)
    gates = nn(grow, rows).astype(BF)
    lane64 = iota((128, 64), 1)
    acc = jnp.zeros((128, 128), F32)
    for kk in range(6):
        gk = nn(one(lane64 == ex[:, kk : kk + 1]), gates)
        gk = jnp.sum(jnp.where(lane == rs[:, kk : kk + 1], gk, 0.0), axis=1, keepdims=True)
        acc = jnp.where(lane == kk, gk, acc)
    gg_ref[...] = acc[:, 0:6]
    ring_sum(14)
    for i in range(4):
        take(dxr.at[i], dx_recv.at[i])
    m = dxr[0].astype(F32) + dxr[1].astype(F32) + dxr[2].astype(F32) + dxr[3].astype(F32)
    tl = got[256:384, 0:64] + got[384:512, 64:128]
    evn = jnp.concatenate([m[:, 0:128] + got[0:128], m[:, 128:256] + got[128:256], m[:, 256:320] + tl], axis=1)
    od = jnp.concatenate([m[:, 64:128] + tl, m[:, 128:256] + got[0:128], m[:, 256:384] + got[128:256]], axis=1)
    gx_ref[...] = jnp.where(is_even, evn, od).astype(BF)

    ring_sum(15)
    ring_sum(16)
    ring_sum(17)
    for t in range(5):
        cols = slice(t * 128, (t + 1) * 128)
        gsg_ref[:, cols] = fo[t * 3]
        gsu_ref[:, cols] = fo[t * 3 + 1]
        gsd_ref[:, cols] = fo[t * 3 + 2]

    for i in range(4):
        own = jnp.logical_and(x == i, y == x)

        @pl.when(jnp.logical_not(own))
        def _():
            take(tx, tok_send.at[i])

        take(xs.at[i, c], tsib_send.at[i])
        own2 = jnp.logical_and(x == y, y == i)

        @pl.when(jnp.logical_not(own2))
        def _():
            take(dxf.at[i], dx_send.at[i])

    pbf = pb.reshape(64, 32, 128)
    take(pbf.at[0:63], disp_send)
    backf = back.reshape(64, 16, 128)
    take(backf.at[0:63], b_send)
    for o in range(1, 4):
        take(sp.at[0], y_send.at[o])
        take(sdall.at[0], y2_send.at[o])
    dx_sib.wait_send()
    for k in range(8):
        for n in range(3):
            take(rall.at[0, 0, k], ag_send.at[k, n])
        for n in range(4):
            take(rall.at[0, 0, k], as_send.at[k, n])
    for h in range(2):
        for o in range(4):
            take(s1.at[h, 0], c_send.at[h, o])
        for o in range(1, 4):
            take(s2.at[h, 0], r_send.at[h, o])
    for q in range(8):
        take(arr.at[0], rr_send.at[q])
        take(fo.at[0], br_send.at[q])
    for q in range(7):
        take(arl.at[0], rl_send.at[q])
        take(fo.at[0], bl_send.at[q])


def on_device(*args):
    sem = pltpu.SemaphoreType.DMA
    vm = pltpu.VMEM
    out_shape = (
        jax.ShapeDtypeStruct((128, 320), BF),
        jax.ShapeDtypeStruct((128, 6), F32),
        jax.ShapeDtypeStruct((192, 640), BF),
        jax.ShapeDtypeStruct((192, 640), BF),
        jax.ShapeDtypeStruct((192, 640), BF),
        jax.ShapeDtypeStruct((1, 96, 2560), BF),
        jax.ShapeDtypeStruct((1, 96, 2560), BF),
        jax.ShapeDtypeStruct((1, 96, 2560), BF),
    )
    scratch = [
        vm((128, 640), BF),
        vm((16, 4, 32, 128), BF),
        vm((16, 4, 32, 128), BF),
        vm((768, 128), BF),
        vm((288, 256), BF),
        vm((128, 240), BF),
        vm((4, 2, 8, 48, 640), BF),
        vm((384, 128), F32),
        vm((384, 2560), BF),
        vm((384, 2560), BF),
        vm((192, 2560), BF),
        vm((384, 192), BF),
        vm((384, 96), BF),
        vm((2, 8, 4, 128, 128), BF),
        vm((2, 4, 4, 128, 128), BF),
        vm((2, 4, 4, 128, 128), BF),
        vm((2, 4, 4, 128, 128), BF),
        vm((2, 4, 8, 16, 128), BF),
        vm((16, 4, 16, 128), BF),
        vm((192, 2560), BF),
        vm((4, 2, 128, 640), BF),
        vm((512, 640), BF),
        vm((512, 640), BF),
        vm((384, 640), BF),
        vm((4, 128, 640), BF),
        vm((4, 128, 640), BF),
        vm((4, 128, 640), BF),
        vm((2, 4, 128, 384), BF),
        vm((4, 128, 384), BF),
        vm((4, 128, 384), BF),
        vm((4, 128, 384), BF),
        vm((16, 192, 128), BF),
        vm((8, 192, 128), BF),
        vm((7, 192, 128), BF),
        vm((16, 192, 128), BF),
        sem((4,)), sem((4,)), sem((4,)), sem((4,)), sem, sem((8,)),
        sem((8, 3)), sem((8, 3)), sem((8, 4)), sem((8, 4)),
        sem((4,)), sem((4,)), sem((4,)), sem((4,)),
        sem, sem, sem((4,)), sem((4,)),
        sem((8,)), sem((8,)), sem((7,)), sem((7,)),
        sem((8,)), sem((8,)), sem((7,)), sem((7,)),
        sem((2, 4)), sem((2, 4)), sem((2, 4)), sem((2, 4)), sem, sem,
    ]
    return pl.pallas_call(
        kernel,
        out_shape=out_shape,
        in_specs=[pl.BlockSpec(memory_space=pltpu.VMEM)] * 11,
        out_specs=tuple([pl.BlockSpec(memory_space=pltpu.VMEM)] * 8),
        scratch_shapes=scratch,
        compiler_params=pltpu.CompilerParams(
            collective_id=0, has_side_effects=True, vmem_limit_bytes=56 * 1024 * 1024
        ),
        cost_estimate=pl.CostEstimate(flops=3_000_000_000, bytes_accessed=6_000_000, transcendentals=100_000),
    )(*args)


def solution(mesh):
    in_specs = (
        P(("node", "dp"), "local"),
        P(("node", "dp"), "local"),
        P(("node", "dp"), None),
        P(("node", "dp"), None),
        P(("node", "dp"), None),
        P("local", "dp"),
        P("local", "dp"),
        P("local", "dp"),
        P(("node", "dp"), "local", None),
        P(("node", "dp"), "local", None),
        P(("node", "dp"), "local", None),
    )
    out_specs = (
        P(("node", "dp"), "local"),
        P(("node", "dp"), None),
        P("local", "dp"),
        P("local", "dp"),
        P("local", "dp"),
        P(("node", "dp"), "local", None),
        P(("node", "dp"), "local", None),
        P(("node", "dp"), "local", None),
    )
    return jax.shard_map(
        on_device, mesh=mesh, in_specs=in_specs, out_specs=out_specs, check_vma=False
    )
```

```python
import jax
import jax.numpy as jnp
from jax import lax
from jax.experimental import pallas as pl
from jax.experimental.pallas import tpu as pltpu
from jax.sharding import PartitionSpec as P

BF = jnp.bfloat16
F32 = jnp.float32
MESH = pl.DeviceIdType.MESH


def nt(a, b):
    return lax.dot_general(a, b, (((1,), (1,)), ((), ())), preferred_element_type=F32)


def nn(a, b):
    return lax.dot_general(a, b, (((1,), (0,)), ((), ())), preferred_element_type=F32)


def tn(a, b):
    return lax.dot_general(a, b, (((0,), (0,)), ((), ())), preferred_element_type=F32)


def iota(shape, dim):
    return lax.broadcasted_iota(jnp.int32, shape, dim)


def sixth(v):
    return lax.shift_right_arithmetic(v * 43, 8)


def one(mask):
    return jnp.where(mask, 1.0, 0.0).astype(BF)


def take(ref, sem):
    pltpu.make_async_copy(ref, ref, sem).wait()


def kernel(
    x_ref, dy_ref, gv_ref, re_ref, rs_ref, sg_ref, su_ref, sd_ref, eg_ref, eu_ref, ed_ref,
    gx_ref, gg_ref, gsg_ref, gsu_ref, gsd_ref, neg_ref, neu_ref, ned_ref,
    tx, pb, pr, vcat, qm, qr, rall, qv, xf, df, wgu, dab, hq, pkb, s1, s2, s3, ret, back, rd,
    xs, xa, da, wsg, sp, r2, sdall, dxp, dxs, dxf, dxr, gp, arr, arl, fo, selm,
    tok_send, tok_recv, tsib_send, tsib_recv, disp_send, disp_recv,
    ag_send, ag_recv, as_send, as_recv, y_send, y_recv, y2_send, y2_recv,
    ds_send, ds_recv, dx_send, dx_recv, rr_send, rr_recv, rl_send, rl_recv,
    br_send, br_recv, bl_send, bl_recv, c_send, c_recv, r_send, r_recv, b_send, b_recv,
):
    z = lax.axis_index("node")
    y = lax.axis_index("dp")
    l = lax.axis_index("local")
    x = l // 2
    c = l % 2
    oc = 1 - c

    def loc(xx, cc):
        return xx * 2 + cc

    bar = pltpu.get_barrier_semaphore()

    def greet(zz, ll, yy):
        pl.semaphore_signal(bar, inc=1, device_id=(zz, ll, yy), device_id_type=MESH)

    greet(z, loc(x, oc), y)

    def greet_plane(i, _):
        p = (x * 4 + y + 1 + i) % 16
        greet(z, loc(p // 4, c), p % 4)
        return 0

    lax.fori_loop(0, 15, greet_plane, 0)

    def greet_z(i, _):
        greet((z + 1 + i // 4) % 16, l, i % 4)
        return 0

    lax.fori_loop(0, 60, greet_z, 0)

    lane = iota((128, 128), 1)
    row = iota((128, 128), 0)
    eye = one(lane == row)
    xv = nt(eye, x_ref[...])
    dv = nt(eye, dy_ref[...])
    even = jnp.concatenate([xv, dv[:, 256:320], dv[:, :256]], axis=1)
    odd = jnp.concatenate([xv[:, 64:320], dv[:, 0:64], xv[:, 0:64], dv[:, 64:320]], axis=1)
    is_even = c == 0
    tx[...] = jnp.where(is_even, even, odd).astype(BF)

    re_t = re_ref[...]
    rs_t = rs_ref[...]
    nd = lax.shift_right_arithmetic(re_t * 205, 11)
    e_t = jnp.where(rs_t >= 0, lax.rem(nd + 16 - z, 16) * 4 + (re_t - nd * 10), -1)
    p_t = jnp.where(rs_t >= 0, e_t * 6 + rs_t, -1)
    e_f = e_t.astype(F32)
    s_f = rs_t.astype(F32)
    g_f = gv_ref[...].astype(F32)
    both = jnp.zeros((128, 128), F32)
    for k in range(6):
        both = jnp.where(row == k, e_f[k : k + 1, :], both)
        both = jnp.where(row == 8 + k, s_f[k : k + 1, :], both)
        both = jnp.where(row == 16 + k, g_f[k : k + 1, :], both)
    turned = both.T
    turned_i = turned.astype(jnp.int32)
    ex = turned_i[:, 0:6]
    rs = turned_i[:, 8:14]
    for k in range(6):
        vcat[k * 128 : (k + 1) * 128, :] = jnp.where(
            lane == rs[:, k : k + 1], turned[:, 16 + k : 17 + k], 0.0
        ).astype(BF)

    pl.semaphore_wait(bar, 76)

    for i in range(4):
        own = jnp.logical_and(x == i, y == x)

        @pl.when(own)
        def _():
            pltpu.make_async_copy(tx, xs.at[y, c], tok_recv.at[y]).start()

        @pl.when(jnp.logical_not(own))
        def _():
            pltpu.make_async_remote_copy(
                tx, xs.at[y, c], tok_send.at[i], tok_recv.at[y],
                device_id=(z, loc(i, c), x), device_id_type=MESH,
            ).start()

    ry = lax.shift_right_arithmetic(row, 5)
    rr = row & 31
    rt = sixth(rr)
    rc = rr - rt * 6

    def chunk(i, _):
        k = i // 2
        h = i % 2
        dz = (8 - k) * (1 - h) + (8 + k) * ((k + 7) // 8) * h
        code = jnp.where(rr < 30, (dz * 4 + ry) * 6 + rc, -7)
        ecode = jnp.where(rr == 30, dz * 4 + ry, -7)
        hit = code == p_t[0:1, :]
        for kk in range(1, 6):
            hit = jnp.logical_or(hit, code == p_t[kk : kk + 1, :])
        prod = nn(one(hit), tx[...])
        out = nn(
            jnp.concatenate([one(ecode == e_t[kk : kk + 1, :]) for kk in range(6)], axis=1), vcat[...]
        )
        for t in range(5):
            out = out + jnp.where(rt == t, prod[:, t * 128 : (t + 1) * 128], 0.0)
        pb[dz] = out.astype(BF).reshape(4, 32, 128)
        for j in range(4):
            own = jnp.logical_and(dz == 0, y == j)

            @pl.when(own)
            def _():
                pltpu.make_async_copy(pb.at[dz, j], pr.at[dz, y], disp_recv.at[k]).start()

            @pl.when(jnp.logical_not(own))
            def _():
                pltpu.make_async_remote_copy(
                    pb.at[dz, j], pr.at[dz, y], disp_send, disp_recv.at[k],
                    device_id=((z + dz) % 16, l, j), device_id_type=MESH,
                ).start()
        return 0

    lax.fori_loop(0, 16, chunk, 0)

    col = iota((288, 256), 1)
    qrow = iota((288, 256), 0)
    cr = col & 31
    ct = sixth(cr)
    cb = lax.shift_right_arithmetic(col, 5) * 6
    dest = ct * 48 + cb + (cr - ct * 6)
    gate_row = qrow - 240 - cb
    qm[...] = one(
        jnp.logical_or(
            jnp.logical_and(cr < 30, qrow == dest),
            jnp.logical_and(cr == 30, jnp.logical_and(gate_row >= 0, gate_row < 6)),
        )
    )
    orow = iota((128, 240), 0)
    ocol = iota((128, 240), 1)
    og = lax.shift_right_arithmetic(orow, 4) * 6
    orr = orow & 15
    keep = jnp.logical_and(orr < 6, ocol == og + orr)
    keep = jnp.logical_or(keep, jnp.logical_and(jnp.logical_and(orr >= 6, orr < 12), ocol == 48 + og + orr - 6))
    tail = jnp.logical_and(orr >= 12, orr < 15)
    keep = jnp.logical_or(keep, jnp.logical_and(tail, ocol == 96 + og + orr - 12))
    keep = jnp.logical_or(keep, jnp.logical_and(tail, ocol == 144 + og + orr - 9))
    goff = ocol - 192 - og
    keep = jnp.logical_or(keep, jnp.logical_and(orr == 15, jnp.logical_and(goff >= 0, goff < 6)))
    qr[...] = one(keep)
    wgu[0:96, :] = eg_ref[0]
    wgu[96:192, :] = eu_ref[0]
    wsg[0:192, :] = sg_ref[...]
    wsg[192:384, :] = su_ref[...]

    lane48 = iota((48, 128), 1)
    row48 = iota((48, 128), 0)
    low48 = lane48 < 64
    c48 = row48 - sixth(row48) * 6

    zr = (z + 1) % 16
    zl = (z + 15) % 16

    def send_right(src, dst, ss, rsem):
        pltpu.make_async_remote_copy(
            src, dst, ss, rsem, device_id=(zr, l, y), device_id_type=MESH
        ).start()

    def send_left(src, dst, ss, rsem):
        pltpu.make_async_remote_copy(
            src, dst, ss, rsem, device_id=(zl, l, y), device_id_type=MESH
        ).start()

    def ring_sum(s):
        for u in range(2):
            ring_part(s, u, pl.ds(u * 96, 96))

    def ring_part(s, u, w):
        if s == 1:
            send_right(gp.at[(z + 8) % 16, w], arr.at[0, w], rr_send.at[0, u], rr_recv.at[0, u])
            send_left(gp.at[(z + 9) % 16, w], arl.at[0, w], rl_send.at[0, u], rl_recv.at[0, u])
            return
        if s <= 8:
            q = s - 2
            take(arr.at[q, w], rr_recv.at[q, u])
            arr[q, w] = (arr[q, w].astype(F32) + gp[(z + 9 - s) % 16, w].astype(F32)).astype(BF)
            send_right(arr.at[q, w], arr.at[q + 1, w], rr_send.at[q + 1, u], rr_recv.at[q + 1, u])
            if s <= 7:
                take(arl.at[q, w], rl_recv.at[q, u])
                arl[q, w] = (arl[q, w].astype(F32) + gp[(z + 8 + s) % 16, w].astype(F32)).astype(BF)
                send_left(arl.at[q, w], arl.at[q + 1, w], rl_send.at[q + 1, u], rl_recv.at[q + 1, u])
            return
        if s == 9:
            take(arr.at[7, w], rr_recv.at[7, u])
            take(arl.at[6, w], rl_recv.at[6, u])
            fo[z, w] = (gp[z, w].astype(F32) + arr[7, w].astype(F32) + arl[6, w].astype(F32)).astype(BF)
        q = s - 9
        if q > 0 and q <= 8:
            take(fo.at[(z + 16 - q) % 16, w], br_recv.at[q - 1, u])
        if q < 8:
            src = fo.at[(z + 16 - q) % 16, w]
            send_right(src, src, br_send.at[q, u], br_recv.at[q, u])
        if q > 0 and q <= 7:
            take(fo.at[(z + q) % 16, w], bl_recv.at[q - 1, u])
        if q < 7:
            src = fo.at[(z + q) % 16, w]
            send_left(src, src, bl_send.at[q, u], bl_recv.at[q, u])

    def unpack(k):
        a = 8 - k
        b = (8 + k) % 16 if k else 0
        take(pr.at[0:2], disp_recv.at[k])
        u = nn(qm[...], jnp.concatenate([pr[a].reshape(128, 128), pr[b].reshape(128, 128)], axis=0))
        for t in range(5):
            rall[x, c, k, :, t * 128 : (t + 1) * 128] = u[t * 48 : (t + 1) * 48].astype(BF)
        q = jnp.sum(jnp.where(lane48 == c48, u[240:288], 0.0), axis=1, keepdims=True)
        qv[k * 48 : (k + 1) * 48, :] = jnp.broadcast_to(q, (48, 128))
        blk = rall.at[x, c, k]
        for n, dx in enumerate((1, 3)):
            pltpu.make_async_remote_copy(
                blk, blk, ag_send.at[k, n], ag_recv.at[k, n],
                device_id=(z, loc((x + dx) % 4, c), y), device_id_type=MESH,
            ).start()
        pltpu.make_async_remote_copy(
            blk, blk, as_send.at[k, 0], as_recv.at[k, 0],
            device_id=(z, loc(x, oc), y), device_id_type=MESH,
        ).start()

    def to_sib(blk, k, n):
        pltpu.make_async_remote_copy(
            blk, blk, as_send.at[k, n], as_recv.at[k, n],
            device_id=(z, loc(x, oc), y), device_id_type=MESH,
        ).start()

    def forward(k):
        left = rall.at[(x + 3) % 4, c, k]
        right = rall.at[(x + 1) % 4, c, k]
        take(left, ag_recv.at[k, 0])
        if k % 2 == 0:
            pltpu.make_async_remote_copy(
                left, left, ag_send.at[k, 2], ag_recv.at[k, 2],
                device_id=(z, loc((x + 1) % 4, c), y), device_id_type=MESH,
            ).start()
        to_sib(left, k, 1)
        take(right, ag_recv.at[k, 1])
        if k % 2 == 1:
            pltpu.make_async_remote_copy(
                right, right, ag_send.at[k, 2], ag_recv.at[k, 2],
                device_id=(z, loc((x + 3) % 4, c), y), device_id_type=MESH,
            ).start()
        to_sib(right, k, 2)

    def across(k):
        far = rall.at[(x + 2) % 4, c, k]
        take(far, ag_recv.at[k, 2])
        to_sib(far, k, 3)

    def settle(k):
        for n, dx in enumerate((0, 3, 1, 2)):
            take(rall.at[(x + dx) % 4, oc, k], as_recv.at[k, n])

    def half(h):
        lo = 192 * h
        rows = slice(lo, lo + 192)
        lane192 = iota((192, 128), 1) < 64
        for p in range(4):
            te = rall[p, 0, 4 * h : 4 * h + 4].reshape(192, 640)
            to = rall[p, 1, 4 * h : 4 * h + 4].reshape(192, 640)
            te_t = te[:, 256:384].astype(F32)
            to_t = to[:, 256:384].astype(F32)
            b = p * 640
            xf[rows, b : b + 256] = te[:, 0:256]
            xf[rows, b + 256 : b + 384] = jnp.where(lane192, te_t, to_t).astype(BF)
            xf[rows, b + 384 : b + 640] = to[:, 0:256]
            df[rows, b : b + 256] = te[:, 384:640]
            df[rows, b + 256 : b + 384] = jnp.where(
                lane192, pltpu.roll(te_t, 64, 1), pltpu.roll(to_t, 64, 1)
            ).astype(BF)
            df[rows, b + 384 : b + 640] = to[:, 384:640]
        ab = nt(xf[rows, :], wgu[...])
        e = nt(df[rows, :], ed_ref[0])
        a = ab[:, 0:96]
        b = ab[:, 96:192]
        sg = 1.0 / (1.0 + jnp.exp(-a))
        sl = a * sg
        hid = sl * b
        gpart = jnp.sum(e * hid, axis=1, keepdims=True)
        q = qv[rows, 0:1]
        qe = q * e
        dab[rows, :] = jnp.concatenate([qe * b * sg * (1.0 + a * (1.0 - sg)), qe * sl], axis=1).astype(BF)
        hq[rows, :] = (q * hid).astype(BF)
        rd[...] = nn(dab[rows, :], wgu[...]).astype(BF)
        for k in range(4):
            r48 = slice(k * 48, (k + 1) * 48)
            g = jnp.where(lane48 == c48, gpart[r48], 0.0).astype(BF)
            zero = jnp.zeros((48, 128), F32)
            cols = []
            for p in range(4):
                t = rd[r48, p * 640 + 256 : p * 640 + 384].astype(F32)
                u = pltpu.roll(t, 64, 1)
                for cc in range(2):
                    b = p * 640 + cc * 384
                    first, second = (t, u) if cc == 0 else (u, t)
                    cols.append(
                        jnp.concatenate(
                            [
                                rd[r48, b : b + 128],
                                rd[r48, b + 128 : b + 256],
                                jnp.where(low48, first, zero).astype(BF),
                                jnp.where(low48, zero, second).astype(BF),
                                g,
                            ],
                            axis=0,
                        )
                    )
            packed = nn(qr[...], jnp.concatenate(cols, axis=1)).astype(BF)
            for ll in range(8):
                pkb[h, ll, k] = packed[:, ll * 128 : (ll + 1) * 128]
        for o in (2, 1, 3, 0):
            xx = (x + o) % 4
            pltpu.make_async_remote_copy(
                pkb.at[h, loc(xx, oc)], s1.at[h, xx], c_send.at[h, o], c_recv.at[h, o],
                device_id=(z, loc(x, oc), y), device_id_type=MESH,
            ).start()

    def reduce_pair(h):
        for o in (2, 1, 3, 0):
            xx = (x + o) % 4
            take(s1.at[h, xx], c_recv.at[h, o])
            v = (pkb[h, loc(xx, c)].astype(F32) + s1[h, xx].astype(F32)).astype(BF)
            if o == 0:
                s3[h, x] = v
            else:
                s2[h, xx] = v
                pltpu.make_async_remote_copy(
                    s2.at[h, xx], s3.at[h, x], r_send.at[h, o], r_recv.at[h, o],
                    device_id=(z, loc(xx, c), y), device_id_type=MESH,
                ).start()

    def give_back(h):
        for o in (1, 2, 3):
            take(s3.at[h, (x + 4 - o) % 4], r_recv.at[h, o])
        for k in range(4):
            v = s3[h, 0, k].astype(F32) + s3[h, 1, k].astype(F32)
            v = v + s3[h, 2, k].astype(F32) + s3[h, 3, k].astype(F32)
            ret[h, k] = v.astype(BF).reshape(8, 16, 128)
            kk = 4 * h + k
            for n, dz in enumerate((8 - kk, (8 + kk) % 16 if kk else 0)):
                for j in range(4):
                    src = ret.at[h, k, n * 4 + j]
                    dst = back.at[dz, y]
                    if dz == 0:

                        @pl.when(y == j)
                        def _():
                            pltpu.make_async_copy(src, dst, b_recv).start()

                        @pl.when(y != j)
                        def _():
                            pltpu.make_async_remote_copy(
                                src, dst, b_send, b_recv, device_id=(z, l, j), device_id_type=MESH
                            ).start()

                    else:
                        pltpu.make_async_remote_copy(
                            src, dst, b_send, b_recv,
                            device_id=((z + 16 - dz) % 16, l, j), device_id_type=MESH,
                        ).start()

    def dx_out():
        take(dxs, ds_recv)
        for i in range(4):
            own = jnp.logical_and(x == y, y == i)
            dxf[i] = (dxp[c, i].astype(F32) + dxs[i].astype(F32)).astype(BF)

            @pl.when(own)
            def _():
                pltpu.make_async_copy(dxf.at[i], dxr.at[x], dx_recv.at[x]).start()

            @pl.when(jnp.logical_not(own))
            def _():
                pltpu.make_async_remote_copy(
                    dxf.at[i], dxr.at[x], dx_send.at[i], dx_recv.at[x],
                    device_id=(z, loc(y, c), i), device_id_type=MESH,
                ).start()

    for i in range(4):
        take(xs.at[i, c], tok_recv.at[i])
        pltpu.make_async_remote_copy(
            xs.at[i, c], xs.at[i, c], tsib_send.at[i], tsib_recv.at[i],
            device_id=(z, loc(x, oc), y), device_id_type=MESH,
        ).start()
    jc = iota((128, 1024), 1)
    jr = jc & 15
    jg = lax.shift_right_arithmetic(jc, 4) * 6
    cls_a = jr < 6
    cls_b = jnp.logical_and(jr >= 6, jr < 12)
    cls_t = jnp.logical_and(jr >= 12, jr < 15)
    code = jg + jnp.where(cls_a, jr, jnp.where(cls_b, jr - 6, jr - 12))
    pos = jnp.where(rs >= 0, ex * 6 + rs, -100)
    hit = code == pos[:, 0:1]
    hit2 = code + 3 == pos[:, 0:1]
    for kk in range(1, 6):
        hit = jnp.logical_or(hit, code == pos[:, kk : kk + 1])
        hit2 = jnp.logical_or(hit2, code + 3 == pos[:, kk : kk + 1])
    selm[...] = jnp.concatenate(
        [
            one(jnp.logical_and(hit, cls_a)),
            one(jnp.logical_and(hit, cls_b)),
            one(jnp.logical_and(hit, cls_t)),
            one(jnp.logical_and(hit2, cls_t)),
        ],
        axis=0,
    )
    grow = one(jnp.logical_and(iota((64, 1024), 1) == iota((64, 1024), 0) * 16 + 15, True))
    low128 = lane < 64
    for i in range(4):
        take(xs.at[i, oc], tsib_recv.at[i])
        te = xs[i, 0]
        to = xs[i, 1]
        te_t = te[:, 256:384].astype(F32)
        to_t = to[:, 256:384].astype(F32)
        rows = pl.ds(i * 128, 128)
        xa[rows, 0:256] = te[:, 0:256]
        xa[rows, 256:384] = jnp.where(low128, te_t, to_t).astype(BF)
        xa[rows, 384:640] = to[:, 0:256]
        da[rows, 0:256] = te[:, 384:640]
        da[rows, 256:384] = jnp.where(low128, pltpu.roll(te_t, 64, 1), pltpu.roll(to_t, 64, 1)).astype(BF)
        da[rows, 384:640] = to[:, 384:640]
    for i in range(4):
        rows = pl.ds(i * 128, 128)
        sp[i, :, 0:384] = nt(xa[rows, :], wsg[...]).astype(BF)
        sp[i, :, 384:576] = nt(da[rows, :], sd_ref[...]).astype(BF)
        sp[i, :, 576:640] = jnp.zeros((128, 64), BF)
    for o in range(1, 4):
        to_y = (y + o) % 4
        pltpu.make_async_remote_copy(
            sp.at[to_y], r2.at[y], y_send.at[o], y_recv.at[o],
            device_id=(z, l, to_y), device_id_type=MESH,
        ).start()
    r2[y] = sp[y]
    unpack(0)
    unpack(1)
    forward(0)
    unpack(2)
    forward(1)
    across(0)
    unpack(3)
    forward(2)
    across(1)

    for o in range(1, 4):
        take(r2.at[(y + 4 - o) % 4], y_recv.at[o])
    tot = r2[0].astype(F32) + r2[1].astype(F32) + r2[2].astype(F32) + r2[3].astype(F32)
    sa = tot[:, 0:192]
    sb = tot[:, 192:384]
    se = tot[:, 384:576]
    sig = 1.0 / (1.0 + jnp.exp(-sa))
    sil = sa * sig
    sdall[y] = jnp.concatenate(
        [
            se * sb * sig * (1.0 + sa * (1.0 - sig)),
            se * sil,
            sil * sb,
            jnp.zeros((128, 64), F32),
        ],
        axis=1,
    ).astype(BF)
    for o in range(1, 4):
        pltpu.make_async_remote_copy(
            sdall.at[y], sdall.at[y], y2_send.at[o], y2_recv.at[o],
            device_id=(z, l, (y + o) % 4), device_id_type=MESH,
        ).start()
    unpack(4)
    forward(3)
    across(2)
    unpack(5)
    forward(4)
    across(3)

    for o in range(1, 4):
        take(sdall.at[(y + 4 - o) % 4], y2_recv.at[o])
    sall = sdall[...].reshape(512, 640)
    for t in range(5):
        cols = slice(t * 128, (t + 1) * 128)
        g2 = tn(sall[:, 0:384], xa[:, cols])
        g1 = tn(sall[:, 384:640], da[:, cols])
        gp[t * 3] = g2[0:192].astype(BF)
        gp[t * 3 + 1] = g2[192:384].astype(BF)
        gp[t * 3 + 2] = g1[0:192].astype(BF)
    gp[15] = jnp.zeros((192, 128), BF)

    ring_sum(1)
    unpack(6)
    forward(5)
    across(4)
    unpack(7)
    forward(6)
    across(5)
    ring_sum(2)
    for k in range(4):
        settle(k)
    half(0)
    ring_sum(3)
    forward(7)
    across(6)
    across(7)
    ring_sum(4)
    reduce_pair(0)
    for k in range(4, 8):
        settle(k)
    ring_sum(5)
    half(1)
    ring_sum(6)
    give_back(0)
    ring_sum(7)
    reduce_pair(1)
    ring_sum(8)
    for i in range(4):
        part = nn(sall[i * 128 : (i + 1) * 128, 0:384], wsg[...]).astype(BF)
        dxp[0, i] = part[:, 0:384]
        dxp[1, i] = part[:, 256:640]
    pltpu.make_async_remote_copy(
        dxp.at[oc], dxs, ds_send, ds_recv, device_id=(z, loc(x, oc), y), device_id_type=MESH
    ).start()

    ring_sum(9)
    give_back(1)
    ring_sum(10)
    dx_out()
    ring_sum(11)

    def weight_grads(i, _):
        cols = pl.ds(pl.multiple_of(i * 640, 128), 640)
        g2 = tn(dab[...], xf[:, cols])
        neg_ref[0, :, cols] = g2[0:96].astype(BF)
        neu_ref[0, :, cols] = g2[96:192].astype(BF)
        ned_ref[0, :, cols] = tn(hq[...], df[:, cols]).astype(BF)
        return 0

    lax.fori_loop(0, 2, weight_grads, 0)
    ring_sum(12)
    lax.fori_loop(2, 4, weight_grads, 0)

    ring_sum(13)

    take(back, b_recv)
    rows = back[...].reshape(1024, 128)
    got = nn(selm[...], rows)
    gates = nn(grow, rows).astype(BF)
    lane64 = iota((128, 64), 1)
    acc = jnp.zeros((128, 128), F32)
    for kk in range(6):
        gk = nn(one(lane64 == ex[:, kk : kk + 1]), gates)
        gk = jnp.sum(jnp.where(lane == rs[:, kk : kk + 1], gk, 0.0), axis=1, keepdims=True)
        acc = jnp.where(lane == kk, gk, acc)
    gg_ref[...] = acc.T[0:6, :]
    ring_sum(14)
    for i in range(4):
        take(dxr.at[i], dx_recv.at[i])
    m = dxr[0].astype(F32) + dxr[1].astype(F32) + dxr[2].astype(F32) + dxr[3].astype(F32)
    tl = got[256:384, 0:64] + got[384:512, 64:128]
    evn = jnp.concatenate([m[:, 0:128] + got[0:128], m[:, 128:256] + got[128:256], m[:, 256:320] + tl], axis=1)
    od = jnp.concatenate([m[:, 64:128] + tl, m[:, 128:256] + got[0:128], m[:, 256:384] + got[128:256]], axis=1)
    gx_ref[...] = tn(jnp.where(is_even, evn, od).astype(BF), eye).astype(BF)

    ring_sum(15)
    ring_sum(16)
    ring_sum(17)
    for t in range(5):
        cols = slice(t * 128, (t + 1) * 128)
        gsg_ref[:, cols] = fo[t * 3]
        gsu_ref[:, cols] = fo[t * 3 + 1]
        gsd_ref[:, cols] = fo[t * 3 + 2]

    for i in range(4):
        own = jnp.logical_and(x == i, y == x)

        @pl.when(jnp.logical_not(own))
        def _():
            take(tx, tok_send.at[i])

        take(xs.at[i, c], tsib_send.at[i])
        own2 = jnp.logical_and(x == y, y == i)

        @pl.when(jnp.logical_not(own2))
        def _():
            take(dxf.at[i], dx_send.at[i])

    pbf = pb.reshape(64, 32, 128)
    take(pbf.at[0:63], disp_send)
    backf = back.reshape(64, 16, 128)
    take(backf.at[0:63], b_send)
    for o in range(1, 4):
        take(sp.at[0], y_send.at[o])
        take(sdall.at[0], y2_send.at[o])
    take(dxs, ds_send)
    for k in range(8):
        for n in range(3):
            take(rall.at[0, 0, k], ag_send.at[k, n])
        for n in range(4):
            take(rall.at[0, 0, k], as_send.at[k, n])
    for h in range(2):
        for o in range(4):
            take(s1.at[h, 0], c_send.at[h, o])
        for o in range(1, 4):
            take(s2.at[h, 0], r_send.at[h, o])
    for u in range(2):
        w = pl.ds(u * 96, 96)
        for q in range(8):
            take(arr.at[0, w], rr_send.at[q, u])
            take(fo.at[0, w], br_send.at[q, u])
        for q in range(7):
            take(arl.at[0, w], rl_send.at[q, u])
            take(fo.at[0, w], bl_send.at[q, u])


def hand_over(*refs):
    held, came, left = refs[16:24], refs[24], refs[25]
    inward = [pltpu.make_async_copy(refs[i], held[i], came.at[i]) for i in range(8)]
    outward = [pltpu.make_async_copy(held[i], refs[8 + i], left.at[i]) for i in range(8)]
    for copy in inward:
        copy.start()
    for i in range(8):
        inward[i].wait()
        outward[i].start()
    for copy in outward:
        copy.wait()


def on_device(*args):
    sem = pltpu.SemaphoreType.DMA
    vm = pltpu.VMEM
    out_shape = (
        jax.ShapeDtypeStruct((320, 128), BF),
        jax.ShapeDtypeStruct((6, 128), F32),
        jax.ShapeDtypeStruct((192, 640), BF),
        jax.ShapeDtypeStruct((192, 640), BF),
        jax.ShapeDtypeStruct((192, 640), BF),
        jax.ShapeDtypeStruct((1, 96, 2560), BF),
        jax.ShapeDtypeStruct((1, 96, 2560), BF),
        jax.ShapeDtypeStruct((1, 96, 2560), BF),
    )
    scratch = [
        vm((128, 640), BF),
        vm((16, 4, 32, 128), BF),
        vm((16, 4, 32, 128), BF),
        vm((768, 128), BF),
        vm((288, 256), BF),
        vm((128, 240), BF),
        vm((4, 2, 8, 48, 640), BF),
        vm((384, 128), F32),
        vm((384, 2560), BF),
        vm((384, 2560), BF),
        vm((192, 2560), BF),
        vm((384, 192), BF),
        vm((384, 96), BF),
        vm((2, 8, 4, 128, 128), BF),
        vm((2, 4, 4, 128, 128), BF),
        vm((2, 4, 4, 128, 128), BF),
        vm((2, 4, 4, 128, 128), BF),
        vm((2, 4, 8, 16, 128), BF),
        vm((16, 4, 16, 128), BF),
        vm((192, 2560), BF),
        vm((4, 2, 128, 640), BF),
        vm((512, 640), BF),
        vm((512, 640), BF),
        vm((384, 640), BF),
        vm((4, 128, 640), BF),
        vm((4, 128, 640), BF),
        vm((4, 128, 640), BF),
        vm((2, 4, 128, 384), BF),
        vm((4, 128, 384), BF),
        vm((4, 128, 384), BF),
        vm((4, 128, 384), BF),
        vm((16, 192, 128), BF),
        vm((8, 192, 128), BF),
        vm((7, 192, 128), BF),
        vm((16, 192, 128), BF),
        vm((512, 1024), BF),
        sem((4,)), sem((4,)), sem((4,)), sem((4,)), sem, sem((8,)),
        sem((8, 3)), sem((8, 3)), sem((8, 4)), sem((8, 4)),
        sem((4,)), sem((4,)), sem((4,)), sem((4,)),
        sem, sem, sem((4,)), sem((4,)),
        sem((8, 2)), sem((8, 2)), sem((7, 2)), sem((7, 2)),
        sem((8, 2)), sem((8, 2)), sem((7, 2)), sem((7, 2)),
        sem((2, 4)), sem((2, 4)), sem((2, 4)), sem((2, 4)), sem, sem,
    ]
    x, dy, gv, re, rs = [v.T for v in args[:5]]
    outs = pl.pallas_call(
        kernel,
        out_shape=out_shape,
        in_specs=[pl.BlockSpec(memory_space=pltpu.VMEM)] * 11,
        out_specs=tuple([pl.BlockSpec(memory_space=pltpu.VMEM)] * 8),
        scratch_shapes=scratch,
        compiler_params=pltpu.CompilerParams(
            collective_id=0, has_side_effects=True, vmem_limit_bytes=56 * 1024 * 1024
        ),
        cost_estimate=pl.CostEstimate(flops=3_000_000_000, bytes_accessed=6_000_000, transcendentals=100_000),
    )(x, dy, gv, re, rs, *args[5:])
    outs = pl.pallas_call(
        hand_over,
        out_shape=out_shape,
        in_specs=[pl.BlockSpec(memory_space=pl.ANY)] * 8,
        out_specs=tuple([pl.BlockSpec(memory_space=pl.ANY)] * 8),
        scratch_shapes=[vm(v.shape, v.dtype) for v in out_shape] + [sem((8,)), sem((8,))],
        compiler_params=pltpu.CompilerParams(vmem_limit_bytes=60 * 1024 * 1024),
        cost_estimate=pl.CostEstimate(flops=0, bytes_accessed=5_000_000, transcendentals=0),
    )(*outs)
    return (outs[0].T, outs[1].T, *outs[2:])


def solution(mesh):
    in_specs = (
        P(("node", "dp"), "local"),
        P(("node", "dp"), "local"),
        P(("node", "dp"), None),
        P(("node", "dp"), None),
        P(("node", "dp"), None),
        P("local", "dp"),
        P("local", "dp"),
        P("local", "dp"),
        P(("node", "dp"), "local", None),
        P(("node", "dp"), "local", None),
        P(("node", "dp"), "local", None),
    )
    out_specs = (
        P(("node", "dp"), "local"),
        P(("node", "dp"), None),
        P("local", "dp"),
        P("local", "dp"),
        P("local", "dp"),
        P(("node", "dp"), "local", None),
        P(("node", "dp"), "local", None),
        P(("node", "dp"), "local", None),
    )
    return jax.shard_map(
        on_device, mesh=mesh, in_specs=in_specs, out_specs=out_specs, check_vma=False
    )
```

```python
import jax
import jax.numpy as jnp
from jax import lax
from jax.experimental import pallas as pl
from jax.experimental.pallas import tpu as pltpu
from jax.sharding import PartitionSpec as P

BF = jnp.bfloat16
F32 = jnp.float32
MESH = pl.DeviceIdType.MESH


def nt(a, b):
    return lax.dot_general(a, b, (((1,), (1,)), ((), ())), preferred_element_type=F32)


def nn(a, b):
    return lax.dot_general(a, b, (((1,), (0,)), ((), ())), preferred_element_type=F32)


def tn(a, b):
    return lax.dot_general(a, b, (((0,), (0,)), ((), ())), preferred_element_type=F32)


def iota(shape, dim):
    return lax.broadcasted_iota(jnp.int32, shape, dim)


def sixth(v):
    return lax.shift_right_arithmetic(v * 43, 8)


def one(mask):
    return jnp.where(mask, 1.0, 0.0).astype(BF)


def take(ref, sem):
    pltpu.make_async_copy(ref, ref, sem).wait()


def kernel(
    x_ref, dy_ref, gv_ref, re_ref, rs_ref, sg_ref, su_ref, sd_ref, eg_ref, eu_ref, ed_ref,
    gx_ref, gg_ref, gsg_ref, gsu_ref, gsd_ref, neg_ref, neu_ref, ned_ref,
    tx, pb, pr, vcat, qm, qr, rall, qv, xf, df, wgu, dab, hq, pkb, s1, s2, s3, ret, back, rd,
    xs, xa, da, wsg, sp, r2, sdall, dxp, dxs, dxf, dxr, gp, ra, ro, la, lo, fo, selm,
    tok_send, tok_recv, tsib_send, tsib_recv, disp_send, disp_recv,
    ag_send, ag_recv, as_send, as_recv, y_send, y_recv, y2_send, y2_recv,
    ds_send, ds_recv, dx_send, dx_recv, ra_send, ra_recv, ro_send, ro_recv,
    la_send, la_recv, lo_send, lo_recv, be_send, be_recv, bo_send, bo_recv,
    le_send, le_recv, ll_send, ll_recv, c_send, c_recv, r_send, r_recv, b_send, b_recv,
):
    z = lax.axis_index("node")
    y = lax.axis_index("dp")
    l = lax.axis_index("local")
    x = l // 2
    c = l % 2
    oc = 1 - c

    def loc(xx, cc):
        return xx * 2 + cc

    bar = pltpu.get_barrier_semaphore()

    def greet(zz, ll, yy):
        pl.semaphore_signal(bar, inc=1, device_id=(zz, ll, yy), device_id_type=MESH)

    greet(z, loc(x, oc), y)

    def greet_plane(i, _):
        p = (x * 4 + y + 1 + i) % 16
        greet(z, loc(p // 4, c), p % 4)
        return 0

    lax.fori_loop(0, 15, greet_plane, 0)

    def greet_z(i, _):
        greet((z + 1 + i // 4) % 16, l, i % 4)
        return 0

    lax.fori_loop(0, 60, greet_z, 0)

    lane = iota((128, 128), 1)
    row = iota((128, 128), 0)
    eye = one(lane == row)
    xv = nt(eye, x_ref[...])
    dv = nt(eye, dy_ref[...])
    even = jnp.concatenate([xv, dv[:, 256:320], dv[:, :256]], axis=1)
    odd = jnp.concatenate([xv[:, 64:320], dv[:, 0:64], xv[:, 0:64], dv[:, 64:320]], axis=1)
    is_even = c == 0
    tx[...] = jnp.where(is_even, even, odd).astype(BF)

    re_t = re_ref[...]
    rs_t = rs_ref[...]
    nd = lax.shift_right_arithmetic(re_t * 205, 11)
    e_t = jnp.where(rs_t >= 0, lax.rem(nd + 16 - z, 16) * 4 + (re_t - nd * 10), -1)
    p_t = jnp.where(rs_t >= 0, e_t * 6 + rs_t, -1)
    e_f = e_t.astype(F32)
    s_f = rs_t.astype(F32)
    g_f = gv_ref[...].astype(F32)
    both = jnp.zeros((128, 128), F32)
    for k in range(6):
        both = jnp.where(row == k, e_f[k : k + 1, :], both)
        both = jnp.where(row == 8 + k, s_f[k : k + 1, :], both)
        both = jnp.where(row == 16 + k, g_f[k : k + 1, :], both)
    turned = both.T
    turned_i = turned.astype(jnp.int32)
    ex = turned_i[:, 0:6]
    rs = turned_i[:, 8:14]
    for k in range(6):
        vcat[k * 128 : (k + 1) * 128, :] = jnp.where(
            lane == rs[:, k : k + 1], turned[:, 16 + k : 17 + k], 0.0
        ).astype(BF)

    pl.semaphore_wait(bar, 76)

    for i in range(4):
        own = jnp.logical_and(x == i, y == x)

        @pl.when(own)
        def _():
            pltpu.make_async_copy(tx, xs.at[y, c], tok_recv.at[y]).start()

        @pl.when(jnp.logical_not(own))
        def _():
            pltpu.make_async_remote_copy(
                tx, xs.at[y, c], tok_send.at[i], tok_recv.at[y],
                device_id=(z, loc(i, c), x), device_id_type=MESH,
            ).start()

    ry = lax.shift_right_arithmetic(row, 5)
    rr = row & 31
    rt = sixth(rr)
    rc = rr - rt * 6

    def chunk(i, _):
        k = i // 2
        h = i % 2
        dz = (8 - k) * (1 - h) + (8 + k) * ((k + 7) // 8) * h
        code = jnp.where(rr < 30, (dz * 4 + ry) * 6 + rc, -7)
        ecode = jnp.where(rr == 30, dz * 4 + ry, -7)
        hit = code == p_t[0:1, :]
        for kk in range(1, 6):
            hit = jnp.logical_or(hit, code == p_t[kk : kk + 1, :])
        prod = nn(one(hit), tx[...])
        out = nn(
            jnp.concatenate([one(ecode == e_t[kk : kk + 1, :]) for kk in range(6)], axis=1), vcat[...]
        )
        for t in range(5):
            out = out + jnp.where(rt == t, prod[:, t * 128 : (t + 1) * 128], 0.0)
        pb[dz] = out.astype(BF).reshape(4, 32, 128)
        for j in range(4):
            own = jnp.logical_and(dz == 0, y == j)

            @pl.when(own)
            def _():
                pltpu.make_async_copy(pb.at[dz, j], pr.at[dz, y], disp_recv.at[k]).start()

            @pl.when(jnp.logical_not(own))
            def _():
                pltpu.make_async_remote_copy(
                    pb.at[dz, j], pr.at[dz, y], disp_send, disp_recv.at[k],
                    device_id=((z + dz) % 16, l, j), device_id_type=MESH,
                ).start()
        return 0

    lax.fori_loop(0, 16, chunk, 0)

    col = iota((288, 256), 1)
    qrow = iota((288, 256), 0)
    cr = col & 31
    ct = sixth(cr)
    cb = lax.shift_right_arithmetic(col, 5) * 6
    dest = ct * 48 + cb + (cr - ct * 6)
    gate_row = qrow - 240 - cb
    qm[...] = one(
        jnp.logical_or(
            jnp.logical_and(cr < 30, qrow == dest),
            jnp.logical_and(cr == 30, jnp.logical_and(gate_row >= 0, gate_row < 6)),
        )
    )
    orow = iota((128, 240), 0)
    ocol = iota((128, 240), 1)
    og = lax.shift_right_arithmetic(orow, 4) * 6
    orr = orow & 15
    keep = jnp.logical_and(orr < 6, ocol == og + orr)
    keep = jnp.logical_or(keep, jnp.logical_and(jnp.logical_and(orr >= 6, orr < 12), ocol == 48 + og + orr - 6))
    tail = jnp.logical_and(orr >= 12, orr < 15)
    keep = jnp.logical_or(keep, jnp.logical_and(tail, ocol == 96 + og + orr - 12))
    keep = jnp.logical_or(keep, jnp.logical_and(tail, ocol == 144 + og + orr - 9))
    goff = ocol - 192 - og
    keep = jnp.logical_or(keep, jnp.logical_and(orr == 15, jnp.logical_and(goff >= 0, goff < 6)))
    qr[...] = one(keep)
    wgu[0:96, :] = eg_ref[0]
    wgu[96:192, :] = eu_ref[0]
    wsg[0:192, :] = sg_ref[...]
    wsg[192:384, :] = su_ref[...]

    lane48 = iota((48, 128), 1)
    row48 = iota((48, 128), 0)
    low48 = lane48 < 64
    c48 = row48 - sixth(row48) * 6

    def hop(src, dst, ss, rsem, by):
        pltpu.make_async_remote_copy(
            src, dst, ss, rsem, device_id=((z + 16 + by) % 16, l, y), device_id_type=MESH
        ).start()

    def ring(s):
        for u in range(2):
            ring_part(s, u, pl.ds(u * 96, 96))

    def term(d, w):
        return gp[(z + 16 + d) % 16, w].astype(F32)

    def odd_right(i, u, w):
        hop(gp.at[(z + 7 - 2 * i) % 16, w], ro.at[i, w], ro_send.at[i, u], ro_recv.at[i, u], 1)

    def odd_left(i, u, w):
        hop(gp.at[(z + 9 + 2 * i) % 16, w], lo.at[i, w], lo_send.at[i, u], lo_recv.at[i, u], -1)

    def ring_part(s, u, w):
        if s == 0:
            hop(gp.at[(z + 8) % 16, w], ra.at[0, w], ra_send.at[0, u], ra_recv.at[0, u], 2)
            odd_left(0, u, w)
            odd_right(0, u, w)
            odd_left(1, u, w)
            odd_right(1, u, w)
        elif s <= 3:
            q = s - 1
            take(lo.at[q, w], lo_recv.at[q, u])
            v = lo[q, w].astype(F32) + term(2 * s - 8, w)
            if s > 1:
                take(la.at[s - 2, w], la_recv.at[s - 2, u])
                v = v + la[s - 2, w].astype(F32)
            lo[q, w] = v.astype(BF)
            hop(lo.at[q, w], la.at[q, w], la_send.at[q, u], la_recv.at[q, u], -2)
            take(ra.at[q, w], ra_recv.at[q, u])
            take(ro.at[q, w], ro_recv.at[q, u])
            v = ra[q, w].astype(F32) + ro[q, w].astype(F32) + term(8 - 2 * s, w)
            ra[q, w] = v.astype(BF)
            hop(ra.at[q, w], ra.at[s, w], ra_send.at[s, u], ra_recv.at[s, u], 2)
            if s < 3:
                odd_left(s + 1, u, w)
                odd_right(s + 1, u, w)
        elif s <= 7:
            p = s - 4
            if p == 0:
                take(la.at[2, w], la_recv.at[2, u])
                take(lo.at[3, w], lo_recv.at[3, u])
                take(ra.at[3, w], ra_recv.at[3, u])
                take(ro.at[3, w], ro_recv.at[3, u])
                v = term(0, w) + ra[3, w].astype(F32) + ro[3, w].astype(F32)
                v = v + la[2, w].astype(F32) + lo[3, w].astype(F32)
                fo[z, w] = v.astype(BF)
            src = fo.at[(z + 16 - 2 * p) % 16, w]
            if p:
                take(src, be_recv.at[p - 1, u])
            hop(src, src, be_send.at[p, u], be_recv.at[p, u], 2)
            src2 = fo.at[(z + 2 * p) % 16, w]
            if p:
                take(src2, le_recv.at[p - 1, u])
            if p < 3:
                hop(src2, src2, le_send.at[p, u], le_recv.at[p, u], -2)
            hop(src, src, bo_send.at[p, u], bo_recv.at[p, u], 1)
            hop(src2, src2, ll_send.at[p, u], ll_recv.at[p, u], -1)
        else:
            take(fo.at[(z + 8) % 16, w], be_recv.at[3, u])
            for p in range(4):
                take(fo.at[(z + 15 - 2 * p) % 16, w], bo_recv.at[p, u])
                take(fo.at[(z + 1 + 2 * p) % 16, w], ll_recv.at[p, u])

    def unpack(k):
        a = 8 - k
        b = (8 + k) % 16 if k else 0
        take(pr.at[0:2], disp_recv.at[k])
        u = nn(qm[...], jnp.concatenate([pr[a].reshape(128, 128), pr[b].reshape(128, 128)], axis=0))
        for t in range(5):
            rall[x, c, k, :, t * 128 : (t + 1) * 128] = u[t * 48 : (t + 1) * 48].astype(BF)
        q = jnp.sum(jnp.where(lane48 == c48, u[240:288], 0.0), axis=1, keepdims=True)
        qv[k * 48 : (k + 1) * 48, :] = jnp.broadcast_to(q, (48, 128))
        blk = rall.at[x, c, k]
        for n, dx in enumerate((1, 3)):
            pltpu.make_async_remote_copy(
                blk, blk, ag_send.at[k, n], ag_recv.at[k, n],
                device_id=(z, loc((x + dx) % 4, c), y), device_id_type=MESH,
            ).start()
        pltpu.make_async_remote_copy(
            blk, blk, as_send.at[k, 0], as_recv.at[k, 0],
            device_id=(z, loc(x, oc), y), device_id_type=MESH,
        ).start()

    def to_sib(blk, k, n):
        pltpu.make_async_remote_copy(
            blk, blk, as_send.at[k, n], as_recv.at[k, n],
            device_id=(z, loc(x, oc), y), device_id_type=MESH,
        ).start()

    def forward(k):
        left = rall.at[(x + 3) % 4, c, k]
        right = rall.at[(x + 1) % 4, c, k]
        take(left, ag_recv.at[k, 0])
        if k % 2 == 0:
            pltpu.make_async_remote_copy(
                left, left, ag_send.at[k, 2], ag_recv.at[k, 2],
                device_id=(z, loc((x + 1) % 4, c), y), device_id_type=MESH,
            ).start()
        to_sib(left, k, 1)
        take(right, ag_recv.at[k, 1])
        if k % 2 == 1:
            pltpu.make_async_remote_copy(
                right, right, ag_send.at[k, 2], ag_recv.at[k, 2],
                device_id=(z, loc((x + 3) % 4, c), y), device_id_type=MESH,
            ).start()
        to_sib(right, k, 2)

    def across(k):
        far = rall.at[(x + 2) % 4, c, k]
        take(far, ag_recv.at[k, 2])
        to_sib(far, k, 3)

    def settle(k):
        for n, dx in enumerate((0, 3, 1, 2)):
            take(rall.at[(x + dx) % 4, oc, k], as_recv.at[k, n])

    def half(h):
        lo = 192 * h
        rows = slice(lo, lo + 192)
        lane192 = iota((192, 128), 1) < 64
        for p in range(4):
            te = rall[p, 0, 4 * h : 4 * h + 4].reshape(192, 640)
            to = rall[p, 1, 4 * h : 4 * h + 4].reshape(192, 640)
            te_t = te[:, 256:384].astype(F32)
            to_t = to[:, 256:384].astype(F32)
            b = p * 640
            xf[rows, b : b + 256] = te[:, 0:256]
            xf[rows, b + 256 : b + 384] = jnp.where(lane192, te_t, to_t).astype(BF)
            xf[rows, b + 384 : b + 640] = to[:, 0:256]
            df[rows, b : b + 256] = te[:, 384:640]
            df[rows, b + 256 : b + 384] = jnp.where(
                lane192, pltpu.roll(te_t, 64, 1), pltpu.roll(to_t, 64, 1)
            ).astype(BF)
            df[rows, b + 384 : b + 640] = to[:, 384:640]
        ab = nt(xf[rows, :], wgu[...])
        e = nt(df[rows, :], ed_ref[0])
        a = ab[:, 0:96]
        b = ab[:, 96:192]
        sg = 1.0 / (1.0 + jnp.exp(-a))
        sl = a * sg
        hid = sl * b
        gpart = jnp.sum(e * hid, axis=1, keepdims=True)
        q = qv[rows, 0:1]
        qe = q * e
        dab[rows, :] = jnp.concatenate([qe * b * sg * (1.0 + a * (1.0 - sg)), qe * sl], axis=1).astype(BF)
        hq[rows, :] = (q * hid).astype(BF)
        rd[...] = nn(dab[rows, :], wgu[...]).astype(BF)
        for k in range(4):
            r48 = slice(k * 48, (k + 1) * 48)
            g = jnp.where(lane48 == c48, gpart[r48], 0.0).astype(BF)
            zero = jnp.zeros((48, 128), F32)
            cols = []
            for p in range(4):
                t = rd[r48, p * 640 + 256 : p * 640 + 384].astype(F32)
                u = pltpu.roll(t, 64, 1)
                for cc in range(2):
                    b = p * 640 + cc * 384
                    first, second = (t, u) if cc == 0 else (u, t)
                    cols.append(
                        jnp.concatenate(
                            [
                                rd[r48, b : b + 128],
                                rd[r48, b + 128 : b + 256],
                                jnp.where(low48, first, zero).astype(BF),
                                jnp.where(low48, zero, second).astype(BF),
                                g,
                            ],
                            axis=0,
                        )
                    )
            packed = nn(qr[...], jnp.concatenate(cols, axis=1)).astype(BF)
            for ll in range(8):
                pkb[h, ll, k] = packed[:, ll * 128 : (ll + 1) * 128]
        for o in (2, 1, 3, 0):
            xx = (x + o) % 4
            pltpu.make_async_remote_copy(
                pkb.at[h, loc(xx, oc)], s1.at[h, xx], c_send.at[h, o], c_recv.at[h, o],
                device_id=(z, loc(x, oc), y), device_id_type=MESH,
            ).start()

    def reduce_pair(h):
        for o in (2, 1, 3, 0):
            xx = (x + o) % 4
            take(s1.at[h, xx], c_recv.at[h, o])
            v = (pkb[h, loc(xx, c)].astype(F32) + s1[h, xx].astype(F32)).astype(BF)
            if o == 0:
                s3[h, x] = v
            else:
                s2[h, xx] = v
                pltpu.make_async_remote_copy(
                    s2.at[h, xx], s3.at[h, x], r_send.at[h, o], r_recv.at[h, o],
                    device_id=(z, loc(xx, c), y), device_id_type=MESH,
                ).start()

    def give_back(h):
        for o in (1, 2, 3):
            take(s3.at[h, (x + 4 - o) % 4], r_recv.at[h, o])
        for k in range(4):
            v = s3[h, 0, k].astype(F32) + s3[h, 1, k].astype(F32)
            v = v + s3[h, 2, k].astype(F32) + s3[h, 3, k].astype(F32)
            ret[h, k] = v.astype(BF).reshape(8, 16, 128)
            kk = 4 * h + k
            for n, dz in enumerate((8 - kk, (8 + kk) % 16 if kk else 0)):
                for j in range(4):
                    src = ret.at[h, k, n * 4 + j]
                    dst = back.at[dz, y]
                    if dz == 0:

                        @pl.when(y == j)
                        def _():
                            pltpu.make_async_copy(src, dst, b_recv).start()

                        @pl.when(y != j)
                        def _():
                            pltpu.make_async_remote_copy(
                                src, dst, b_send, b_recv, device_id=(z, l, j), device_id_type=MESH
                            ).start()

                    else:
                        pltpu.make_async_remote_copy(
                            src, dst, b_send, b_recv,
                            device_id=((z + 16 - dz) % 16, l, j), device_id_type=MESH,
                        ).start()

    def dx_out():
        take(dxs, ds_recv)
        for i in range(4):
            own = jnp.logical_and(x == y, y == i)
            dxf[i] = (dxp[c, i].astype(F32) + dxs[i].astype(F32)).astype(BF)

            @pl.when(own)
            def _():
                pltpu.make_async_copy(dxf.at[i], dxr.at[x], dx_recv.at[x]).start()

            @pl.when(jnp.logical_not(own))
            def _():
                pltpu.make_async_remote_copy(
                    dxf.at[i], dxr.at[x], dx_send.at[i], dx_recv.at[x],
                    device_id=(z, loc(y, c), i), device_id_type=MESH,
                ).start()

    low128 = lane < 64

    def group_in(o):
        i = (y + o) % 4
        take(xs.at[i, c], tok_recv.at[i])
        pltpu.make_async_remote_copy(
            xs.at[i, c], xs.at[i, c], tsib_send.at[i], tsib_recv.at[i],
            device_id=(z, loc(x, oc), y), device_id_type=MESH,
        ).start()

    def group_forward(o):
        i = (y + o) % 4
        take(xs.at[i, oc], tsib_recv.at[i])
        te = xs[i, 0]
        to = xs[i, 1]
        te_t = te[:, 256:384].astype(F32)
        to_t = to[:, 256:384].astype(F32)
        rows = pl.ds(pl.multiple_of(i * 128, 128), 128)
        xa[rows, 0:256] = te[:, 0:256]
        xa[rows, 256:384] = jnp.where(low128, te_t, to_t).astype(BF)
        xa[rows, 384:640] = to[:, 0:256]
        da[rows, 0:256] = te[:, 384:640]
        da[rows, 256:384] = jnp.where(low128, pltpu.roll(te_t, 64, 1), pltpu.roll(to_t, 64, 1)).astype(BF)
        da[rows, 384:640] = to[:, 384:640]
        sp[i, :, 0:384] = nt(xa[rows, :], wsg[...]).astype(BF)
        sp[i, :, 384:576] = nt(da[rows, :], sd_ref[...]).astype(BF)
        sp[i, :, 576:640] = jnp.zeros((128, 64), BF)
        if o:
            pltpu.make_async_remote_copy(
                sp.at[i], r2.at[y], y_send.at[o], y_recv.at[o],
                device_id=(z, l, i), device_id_type=MESH,
            ).start()
        else:
            r2[y] = sp[y]

    group_in(1)
    group_in(3)
    group_forward(1)
    group_in(2)
    group_forward(3)
    group_in(0)
    group_forward(2)
    group_forward(0)
    jc = iota((128, 1024), 1)
    jr = jc & 15
    jg = lax.shift_right_arithmetic(jc, 4) * 6
    cls_a = jr < 6
    cls_b = jnp.logical_and(jr >= 6, jr < 12)
    cls_t = jnp.logical_and(jr >= 12, jr < 15)
    code = jg + jnp.where(cls_a, jr, jnp.where(cls_b, jr - 6, jr - 12))
    pos = jnp.where(rs >= 0, ex * 6 + rs, -100)
    hit = code == pos[:, 0:1]
    hit2 = code + 3 == pos[:, 0:1]
    for kk in range(1, 6):
        hit = jnp.logical_or(hit, code == pos[:, kk : kk + 1])
        hit2 = jnp.logical_or(hit2, code + 3 == pos[:, kk : kk + 1])
    selm[...] = jnp.concatenate(
        [
            one(jnp.logical_and(hit, cls_a)),
            one(jnp.logical_and(hit, cls_b)),
            one(jnp.logical_and(hit, cls_t)),
            one(jnp.logical_and(hit2, cls_t)),
        ],
        axis=0,
    )
    grow = one(jnp.logical_and(iota((64, 1024), 1) == iota((64, 1024), 0) * 16 + 15, True))
    unpack(0)
    unpack(1)
    forward(0)
    unpack(2)
    forward(1)
    across(0)
    unpack(3)
    forward(2)
    across(1)

    for o in range(1, 4):
        take(r2.at[(y + 4 - o) % 4], y_recv.at[o])
    tot = r2[0].astype(F32) + r2[1].astype(F32) + r2[2].astype(F32) + r2[3].astype(F32)
    sa = tot[:, 0:192]
    sb = tot[:, 192:384]
    se = tot[:, 384:576]
    sig = 1.0 / (1.0 + jnp.exp(-sa))
    sil = sa * sig
    sdall[y] = jnp.concatenate(
        [
            se * sb * sig * (1.0 + sa * (1.0 - sig)),
            se * sil,
            sil * sb,
            jnp.zeros((128, 64), F32),
        ],
        axis=1,
    ).astype(BF)
    for o in range(1, 4):
        pltpu.make_async_remote_copy(
            sdall.at[y], sdall.at[y], y2_send.at[o], y2_recv.at[o],
            device_id=(z, l, (y + o) % 4), device_id_type=MESH,
        ).start()
    unpack(4)
    forward(3)
    across(2)
    unpack(5)
    forward(4)
    across(3)

    for o in range(1, 4):
        take(sdall.at[(y + 4 - o) % 4], y2_recv.at[o])
    sall = sdall[...].reshape(512, 640)
    for t in range(5):
        cols = slice(t * 128, (t + 1) * 128)
        g2 = tn(sall[:, 0:384], xa[:, cols])
        g1 = tn(sall[:, 384:640], da[:, cols])
        gp[t * 3] = g2[0:192].astype(BF)
        gp[t * 3 + 1] = g2[192:384].astype(BF)
        gp[t * 3 + 2] = g1[0:192].astype(BF)
    gp[15] = jnp.zeros((192, 128), BF)

    ring(0)
    unpack(6)
    forward(5)
    across(4)
    unpack(7)
    forward(6)
    across(5)
    ring(1)
    for k in range(4):
        settle(k)
    half(0)
    ring(2)
    forward(7)
    across(6)
    across(7)
    reduce_pair(0)
    ring(3)
    for k in range(4, 8):
        settle(k)
    half(1)
    ring(4)
    give_back(0)
    reduce_pair(1)
    ring(5)
    for i in range(4):
        part = nn(sall[i * 128 : (i + 1) * 128, 0:384], wsg[...]).astype(BF)
        dxp[0, i] = part[:, 0:384]
        dxp[1, i] = part[:, 256:640]
    pltpu.make_async_remote_copy(
        dxp.at[oc], dxs, ds_send, ds_recv, device_id=(z, loc(x, oc), y), device_id_type=MESH
    ).start()

    give_back(1)
    ring(6)
    dx_out()

    def weight_grads(i, _):
        cols = pl.ds(pl.multiple_of(i * 640, 128), 640)
        g2 = tn(dab[...], xf[:, cols])
        neg_ref[0, :, cols] = g2[0:96].astype(BF)
        neu_ref[0, :, cols] = g2[96:192].astype(BF)
        ned_ref[0, :, cols] = tn(hq[...], df[:, cols]).astype(BF)
        return 0

    lax.fori_loop(0, 2, weight_grads, 0)
    ring(7)
    lax.fori_loop(2, 4, weight_grads, 0)


    take(back, b_recv)
    rows = back[...].reshape(1024, 128)
    got = nn(selm[...], rows)
    gates = nn(grow, rows).astype(BF)
    lane64 = iota((128, 64), 1)
    acc = jnp.zeros((128, 128), F32)
    for kk in range(6):
        gk = nn(one(lane64 == ex[:, kk : kk + 1]), gates)
        gk = jnp.sum(jnp.where(lane == rs[:, kk : kk + 1], gk, 0.0), axis=1, keepdims=True)
        acc = jnp.where(lane == kk, gk, acc)
    gg_ref[...] = acc.T[0:6, :]
    for i in range(4):
        take(dxr.at[i], dx_recv.at[i])
    m = dxr[0].astype(F32) + dxr[1].astype(F32) + dxr[2].astype(F32) + dxr[3].astype(F32)
    tl = got[256:384, 0:64] + got[384:512, 64:128]
    evn = jnp.concatenate([m[:, 0:128] + got[0:128], m[:, 128:256] + got[128:256], m[:, 256:320] + tl], axis=1)
    od = jnp.concatenate([m[:, 64:128] + tl, m[:, 128:256] + got[0:128], m[:, 256:384] + got[128:256]], axis=1)
    gx_ref[...] = tn(jnp.where(is_even, evn, od).astype(BF), eye).astype(BF)

    ring(8)
    for t in range(5):
        cols = slice(t * 128, (t + 1) * 128)
        gsg_ref[:, cols] = fo[t * 3]
        gsu_ref[:, cols] = fo[t * 3 + 1]
        gsd_ref[:, cols] = fo[t * 3 + 2]

    for i in range(4):
        own = jnp.logical_and(x == i, y == x)

        @pl.when(jnp.logical_not(own))
        def _():
            take(tx, tok_send.at[i])

        take(xs.at[i, c], tsib_send.at[i])
        own2 = jnp.logical_and(x == y, y == i)

        @pl.when(jnp.logical_not(own2))
        def _():
            take(dxf.at[i], dx_send.at[i])

    pbf = pb.reshape(64, 32, 128)
    take(pbf.at[0:63], disp_send)
    backf = back.reshape(64, 16, 128)
    take(backf.at[0:63], b_send)
    for o in range(1, 4):
        take(sp.at[0], y_send.at[o])
        take(sdall.at[0], y2_send.at[o])
    take(dxs, ds_send)
    for k in range(8):
        for n in range(3):
            take(rall.at[0, 0, k], ag_send.at[k, n])
        for n in range(4):
            take(rall.at[0, 0, k], as_send.at[k, n])
    for h in range(2):
        for o in range(4):
            take(s1.at[h, 0], c_send.at[h, o])
        for o in range(1, 4):
            take(s2.at[h, 0], r_send.at[h, o])
    for u in range(2):
        w = pl.ds(u * 96, 96)
        for q in range(4):
            take(fo.at[0, w], ra_send.at[q, u])
            take(fo.at[0, w], ro_send.at[q, u])
            take(fo.at[0, w], lo_send.at[q, u])
            take(fo.at[0, w], be_send.at[q, u])
            take(fo.at[0, w], bo_send.at[q, u])
            take(fo.at[0, w], ll_send.at[q, u])
        for q in range(3):
            take(fo.at[0, w], la_send.at[q, u])
            take(fo.at[0, w], le_send.at[q, u])


def hand_over(*refs):
    held, came, left = refs[16:24], refs[24], refs[25]
    inward = [pltpu.make_async_copy(refs[i], held[i], came.at[i]) for i in range(8)]
    outward = [pltpu.make_async_copy(held[i], refs[8 + i], left.at[i]) for i in range(8)]
    for copy in inward:
        copy.start()
    for i in range(8):
        inward[i].wait()
        outward[i].start()
    for copy in outward:
        copy.wait()


def on_device(*args):
    sem = pltpu.SemaphoreType.DMA
    vm = pltpu.VMEM
    out_shape = (
        jax.ShapeDtypeStruct((320, 128), BF),
        jax.ShapeDtypeStruct((6, 128), F32),
        jax.ShapeDtypeStruct((192, 640), BF),
        jax.ShapeDtypeStruct((192, 640), BF),
        jax.ShapeDtypeStruct((192, 640), BF),
        jax.ShapeDtypeStruct((1, 96, 2560), BF),
        jax.ShapeDtypeStruct((1, 96, 2560), BF),
        jax.ShapeDtypeStruct((1, 96, 2560), BF),
    )
    scratch = [
        vm((128, 640), BF),
        vm((16, 4, 32, 128), BF),
        vm((16, 4, 32, 128), BF),
        vm((768, 128), BF),
        vm((288, 256), BF),
        vm((128, 240), BF),
        vm((4, 2, 8, 48, 640), BF),
        vm((384, 128), F32),
        vm((384, 2560), BF),
        vm((384, 2560), BF),
        vm((192, 2560), BF),
        vm((384, 192), BF),
        vm((384, 96), BF),
        vm((2, 8, 4, 128, 128), BF),
        vm((2, 4, 4, 128, 128), BF),
        vm((2, 4, 4, 128, 128), BF),
        vm((2, 4, 4, 128, 128), BF),
        vm((2, 4, 8, 16, 128), BF),
        vm((16, 4, 16, 128), BF),
        vm((192, 2560), BF),
        vm((4, 2, 128, 640), BF),
        vm((512, 640), BF),
        vm((512, 640), BF),
        vm((384, 640), BF),
        vm((4, 128, 640), BF),
        vm((4, 128, 640), BF),
        vm((4, 128, 640), BF),
        vm((2, 4, 128, 384), BF),
        vm((4, 128, 384), BF),
        vm((4, 128, 384), BF),
        vm((4, 128, 384), BF),
        vm((16, 192, 128), BF),
        vm((4, 192, 128), BF),
        vm((4, 192, 128), BF),
        vm((3, 192, 128), BF),
        vm((4, 192, 128), BF),
        vm((16, 192, 128), BF),
        vm((512, 1024), BF),
        sem((4,)), sem((4,)), sem((4,)), sem((4,)), sem, sem((8,)),
        sem((8, 3)), sem((8, 3)), sem((8, 4)), sem((8, 4)),
        sem((4,)), sem((4,)), sem((4,)), sem((4,)),
        sem, sem, sem((4,)), sem((4,)),
        sem((4, 2)), sem((4, 2)), sem((4, 2)), sem((4, 2)),
        sem((3, 2)), sem((3, 2)), sem((4, 2)), sem((4, 2)),
        sem((4, 2)), sem((4, 2)), sem((4, 2)), sem((4, 2)),
        sem((3, 2)), sem((3, 2)), sem((4, 2)), sem((4, 2)),
        sem((2, 4)), sem((2, 4)), sem((2, 4)), sem((2, 4)), sem, sem,
    ]
    x, dy, gv, re, rs = [v.T for v in args[:5]]
    outs = pl.pallas_call(
        kernel,
        out_shape=out_shape,
        in_specs=[pl.BlockSpec(memory_space=pltpu.VMEM)] * 11,
        out_specs=tuple([pl.BlockSpec(memory_space=pltpu.VMEM)] * 8),
        scratch_shapes=scratch,
        compiler_params=pltpu.CompilerParams(
            collective_id=0, has_side_effects=True, vmem_limit_bytes=56 * 1024 * 1024
        ),
        cost_estimate=pl.CostEstimate(flops=3_000_000_000, bytes_accessed=6_000_000, transcendentals=100_000),
    )(x, dy, gv, re, rs, *args[5:])
    outs = pl.pallas_call(
        hand_over,
        out_shape=out_shape,
        in_specs=[pl.BlockSpec(memory_space=pl.ANY)] * 8,
        out_specs=tuple([pl.BlockSpec(memory_space=pl.ANY)] * 8),
        scratch_shapes=[vm(v.shape, v.dtype) for v in out_shape] + [sem((8,)), sem((8,))],
        compiler_params=pltpu.CompilerParams(vmem_limit_bytes=60 * 1024 * 1024),
        cost_estimate=pl.CostEstimate(flops=0, bytes_accessed=5_000_000, transcendentals=0),
    )(*outs)
    return (outs[0].T, outs[1].T, *outs[2:])


def solution(mesh):
    in_specs = (
        P(("node", "dp"), "local"),
        P(("node", "dp"), "local"),
        P(("node", "dp"), None),
        P(("node", "dp"), None),
        P(("node", "dp"), None),
        P("local", "dp"),
        P("local", "dp"),
        P("local", "dp"),
        P(("node", "dp"), "local", None),
        P(("node", "dp"), "local", None),
        P(("node", "dp"), "local", None),
    )
    out_specs = (
        P(("node", "dp"), "local"),
        P(("node", "dp"), None),
        P("local", "dp"),
        P("local", "dp"),
        P("local", "dp"),
        P(("node", "dp"), "local", None),
        P(("node", "dp"), "local", None),
        P(("node", "dp"), "local", None),
    )
    return jax.shard_map(
        on_device, mesh=mesh, in_specs=in_specs, out_specs=out_specs, check_vma=False
    )
```

```python
import jax
import jax.numpy as jnp
from jax import lax
from jax.experimental import pallas as pl
from jax.experimental.pallas import tpu as pltpu
from jax.sharding import PartitionSpec as P

BF = jnp.bfloat16
F32 = jnp.float32
MESH = pl.DeviceIdType.MESH


def nt(a, b):
    return lax.dot_general(a, b, (((1,), (1,)), ((), ())), preferred_element_type=F32)


def nn(a, b):
    return lax.dot_general(a, b, (((1,), (0,)), ((), ())), preferred_element_type=F32)


def tn(a, b):
    return lax.dot_general(a, b, (((0,), (0,)), ((), ())), preferred_element_type=F32)


def iota(shape, dim):
    return lax.broadcasted_iota(jnp.int32, shape, dim)


def sixth(v):
    return lax.shift_right_arithmetic(v * 43, 8)


def one(mask):
    return jnp.where(mask, 1.0, 0.0).astype(BF)


def take(ref, sem):
    pltpu.make_async_copy(ref, ref, sem).wait()


def kernel(
    x_ref, dy_ref, gv_ref, re_ref, rs_ref, sg_ref, su_ref, sd_ref, eg_ref, eu_ref, ed_ref,
    gx_ref, gg_ref, gsg_ref, gsu_ref, gsd_ref, neg_ref, neu_ref, ned_ref,
    tx, pb, pr, vcat, qm, qr, rall, qv, xf, df, wgu, dab, hq, pkb, s1, s2, s3, ret, back, rd,
    xs, xa, da, wsg, sp, r2, sdall, dxp, dxs, dxf, dxr, gp, ra, ro, la, lo, fo, selm,
    tok_send, tok_recv, tsib_send, tsib_recv, disp_send, disp_recv,
    ag_send, ag_recv, as_send, as_recv, y_send, y_recv, y2_send, y2_recv,
    ds_send, ds_recv, dx_send, dx_recv, ra_send, ra_recv, ro_send, ro_recv,
    la_send, la_recv, lo_send, lo_recv, be_send, be_recv, bo_send, bo_recv,
    le_send, le_recv, ll_send, ll_recv, c_send, c_recv, r_send, r_recv, b_send, b_recv,
):
    z = lax.axis_index("node")
    y = lax.axis_index("dp")
    l = lax.axis_index("local")
    x = l // 2
    c = l % 2
    oc = 1 - c

    def loc(xx, cc):
        return xx * 2 + cc

    bar = pltpu.get_barrier_semaphore()

    def greet(zz, ll, yy):
        pl.semaphore_signal(bar, inc=1, device_id=(zz, ll, yy), device_id_type=MESH)

    greet(z, loc(x, oc), y)

    def greet_plane(i, _):
        p = (x * 4 + y + 1 + i) % 16
        greet(z, loc(p // 4, c), p % 4)
        return 0

    lax.fori_loop(0, 15, greet_plane, 0)

    def greet_z(i, _):
        greet((z + 1 + i // 4) % 16, l, i % 4)
        return 0

    lax.fori_loop(0, 60, greet_z, 0)

    lane = iota((128, 128), 1)
    row = iota((128, 128), 0)
    eye = one(lane == row)
    xv = nt(eye, x_ref[...])
    dv = nt(eye, dy_ref[...])
    even = jnp.concatenate([xv, dv[:, 256:320], dv[:, :256]], axis=1)
    odd = jnp.concatenate([xv[:, 64:320], dv[:, 0:64], xv[:, 0:64], dv[:, 64:320]], axis=1)
    is_even = c == 0
    tx[...] = jnp.where(is_even, even, odd).astype(BF)

    re_t = re_ref[...]
    rs_t = rs_ref[...]
    nd = lax.shift_right_arithmetic(re_t * 205, 11)
    e_t = jnp.where(rs_t >= 0, lax.rem(nd + 16 - z, 16) * 4 + (re_t - nd * 10), -1)
    p_t = jnp.where(rs_t >= 0, e_t * 6 + rs_t, -1)
    e_f = e_t.astype(F32)
    s_f = rs_t.astype(F32)
    g_f = gv_ref[...].astype(F32)
    both = jnp.zeros((128, 128), F32)
    for k in range(6):
        both = jnp.where(row == k, e_f[k : k + 1, :], both)
        both = jnp.where(row == 8 + k, s_f[k : k + 1, :], both)
        both = jnp.where(row == 16 + k, g_f[k : k + 1, :], both)
    turned = both.T
    turned_i = turned.astype(jnp.int32)
    ex = turned_i[:, 0:6]
    rs = turned_i[:, 8:14]
    for k in range(6):
        vcat[k * 128 : (k + 1) * 128, :] = jnp.where(
            lane == rs[:, k : k + 1], turned[:, 16 + k : 17 + k], 0.0
        ).astype(BF)

    pl.semaphore_wait(bar, 76)

    for i in range(4):
        own = jnp.logical_and(x == i, y == x)

        @pl.when(own)
        def _():
            pltpu.make_async_copy(tx, xs.at[y, c], tok_recv.at[y]).start()

        @pl.when(jnp.logical_not(own))
        def _():
            pltpu.make_async_remote_copy(
                tx, xs.at[y, c], tok_send.at[i], tok_recv.at[y],
                device_id=(z, loc(i, c), x), device_id_type=MESH,
            ).start()

    ry = lax.shift_right_arithmetic(row, 5)
    rr = row & 31
    rt = sixth(rr)
    rc = rr - rt * 6

    def chunk(i, _):
        k = i // 2
        h = i % 2
        dz = (8 - k) * (1 - h) + (8 + k) * ((k + 7) // 8) * h
        code = jnp.where(rr < 30, (dz * 4 + ry) * 6 + rc, -7)
        ecode = jnp.where(rr == 30, dz * 4 + ry, -7)
        hit = code == p_t[0:1, :]
        for kk in range(1, 6):
            hit = jnp.logical_or(hit, code == p_t[kk : kk + 1, :])
        prod = nn(one(hit), tx[...])
        out = nn(
            jnp.concatenate([one(ecode == e_t[kk : kk + 1, :]) for kk in range(6)], axis=1), vcat[...]
        )
        for t in range(5):
            out = out + jnp.where(rt == t, prod[:, t * 128 : (t + 1) * 128], 0.0)
        pb[dz] = out.astype(BF).reshape(4, 32, 128)
        for j in range(4):
            own = jnp.logical_and(dz == 0, y == j)

            @pl.when(own)
            def _():
                pltpu.make_async_copy(pb.at[dz, j], pr.at[dz, y], disp_recv.at[k]).start()

            @pl.when(jnp.logical_not(own))
            def _():
                pltpu.make_async_remote_copy(
                    pb.at[dz, j], pr.at[dz, y], disp_send, disp_recv.at[k],
                    device_id=((z + dz) % 16, l, j), device_id_type=MESH,
                ).start()
        return 0

    lax.fori_loop(0, 16, chunk, 0)

    col = iota((288, 256), 1)
    qrow = iota((288, 256), 0)
    cr = col & 31
    ct = sixth(cr)
    cb = lax.shift_right_arithmetic(col, 5) * 6
    dest = ct * 48 + cb + (cr - ct * 6)
    gate_row = qrow - 240 - cb
    qm[...] = one(
        jnp.logical_or(
            jnp.logical_and(cr < 30, qrow == dest),
            jnp.logical_and(cr == 30, jnp.logical_and(gate_row >= 0, gate_row < 6)),
        )
    )
    orow = iota((128, 240), 0)
    ocol = iota((128, 240), 1)
    og = lax.shift_right_arithmetic(orow, 4) * 6
    orr = orow & 15
    keep = jnp.logical_and(orr < 6, ocol == og + orr)
    keep = jnp.logical_or(keep, jnp.logical_and(jnp.logical_and(orr >= 6, orr < 12), ocol == 48 + og + orr - 6))
    tail = jnp.logical_and(orr >= 12, orr < 15)
    keep = jnp.logical_or(keep, jnp.logical_and(tail, ocol == 96 + og + orr - 12))
    keep = jnp.logical_or(keep, jnp.logical_and(tail, ocol == 144 + og + orr - 9))
    goff = ocol - 192 - og
    keep = jnp.logical_or(keep, jnp.logical_and(orr == 15, jnp.logical_and(goff >= 0, goff < 6)))
    qr[...] = one(keep)
    wgu[0:96, :] = eg_ref[0]
    wgu[96:192, :] = eu_ref[0]
    wsg[0:192, :] = sg_ref[...]
    wsg[192:384, :] = su_ref[...]

    lane48 = iota((48, 128), 1)
    row48 = iota((48, 128), 0)
    low48 = lane48 < 64
    c48 = row48 - sixth(row48) * 6

    def hop(src, dst, ss, rsem, by):
        pltpu.make_async_remote_copy(
            src, dst, ss, rsem, device_id=((z + 16 + by) % 16, l, y), device_id_type=MESH
        ).start()

    def ring(s):
        for u in range(2):
            ring_part(s, u, pl.ds(u * 96, 96))

    def term(d, w):
        return gp[(z + 16 + d) % 16, w].astype(F32)

    def odd_right(i, u, w):
        hop(gp.at[(z + 7 - 2 * i) % 16, w], ro.at[i, w], ro_send.at[i, u], ro_recv.at[i, u], 1)

    def odd_left(i, u, w):
        hop(gp.at[(z + 9 + 2 * i) % 16, w], lo.at[i, w], lo_send.at[i, u], lo_recv.at[i, u], -1)

    def ring_part(s, u, w):
        if s == 0:
            hop(gp.at[(z + 8) % 16, w], ra.at[0, w], ra_send.at[0, u], ra_recv.at[0, u], 2)
            odd_left(0, u, w)
            odd_right(0, u, w)
            odd_left(1, u, w)
            odd_right(1, u, w)
        elif s <= 3:
            q = s - 1
            take(lo.at[q, w], lo_recv.at[q, u])
            v = lo[q, w].astype(F32) + term(2 * s - 8, w)
            if s > 1:
                take(la.at[s - 2, w], la_recv.at[s - 2, u])
                v = v + la[s - 2, w].astype(F32)
            lo[q, w] = v.astype(BF)
            hop(lo.at[q, w], la.at[q, w], la_send.at[q, u], la_recv.at[q, u], -2)
            take(ra.at[q, w], ra_recv.at[q, u])
            take(ro.at[q, w], ro_recv.at[q, u])
            v = ra[q, w].astype(F32) + ro[q, w].astype(F32) + term(8 - 2 * s, w)
            ra[q, w] = v.astype(BF)
            hop(ra.at[q, w], ra.at[s, w], ra_send.at[s, u], ra_recv.at[s, u], 2)
            if s < 3:
                odd_left(s + 1, u, w)
                odd_right(s + 1, u, w)
        elif s <= 7:
            p = s - 4
            if p == 0:
                take(la.at[2, w], la_recv.at[2, u])
                take(lo.at[3, w], lo_recv.at[3, u])
                take(ra.at[3, w], ra_recv.at[3, u])
                take(ro.at[3, w], ro_recv.at[3, u])
                v = term(0, w) + ra[3, w].astype(F32) + ro[3, w].astype(F32)
                v = v + la[2, w].astype(F32) + lo[3, w].astype(F32)
                fo[z, w] = v.astype(BF)
            src = fo.at[(z + 16 - 2 * p) % 16, w]
            if p:
                take(src, be_recv.at[p - 1, u])
            hop(src, src, be_send.at[p, u], be_recv.at[p, u], 2)
            src2 = fo.at[(z + 2 * p) % 16, w]
            if p:
                take(src2, le_recv.at[p - 1, u])
            if p < 3:
                hop(src2, src2, le_send.at[p, u], le_recv.at[p, u], -2)
            hop(src, src, bo_send.at[p, u], bo_recv.at[p, u], 1)
            hop(src2, src2, ll_send.at[p, u], ll_recv.at[p, u], -1)
        else:
            take(fo.at[(z + 8) % 16, w], be_recv.at[3, u])
            for p in range(4):
                take(fo.at[(z + 15 - 2 * p) % 16, w], bo_recv.at[p, u])
                take(fo.at[(z + 1 + 2 * p) % 16, w], ll_recv.at[p, u])

    def unpack(k):
        a = 8 - k
        b = (8 + k) % 16 if k else 0
        take(pr.at[0:2], disp_recv.at[k])
        u = nn(qm[...], jnp.concatenate([pr[a].reshape(128, 128), pr[b].reshape(128, 128)], axis=0))
        for t in range(5):
            rall[x, c, k, :, t * 128 : (t + 1) * 128] = u[t * 48 : (t + 1) * 48].astype(BF)
        q = jnp.sum(jnp.where(lane48 == c48, u[240:288], 0.0), axis=1, keepdims=True)
        qv[k * 48 : (k + 1) * 48, :] = jnp.broadcast_to(q, (48, 128))
        blk = rall.at[x, c, k]
        for n, dx in enumerate((1, 3)):
            pltpu.make_async_remote_copy(
                blk, blk, ag_send.at[k, n], ag_recv.at[k, n],
                device_id=(z, loc((x + dx) % 4, c), y), device_id_type=MESH,
            ).start()
        pltpu.make_async_remote_copy(
            blk, blk, as_send.at[k, 0], as_recv.at[k, 0],
            device_id=(z, loc(x, oc), y), device_id_type=MESH,
        ).start()

    def to_sib(blk, k, n):
        pltpu.make_async_remote_copy(
            blk, blk, as_send.at[k, n], as_recv.at[k, n],
            device_id=(z, loc(x, oc), y), device_id_type=MESH,
        ).start()

    def forward(k):
        left = rall.at[(x + 3) % 4, c, k]
        right = rall.at[(x + 1) % 4, c, k]
        take(left, ag_recv.at[k, 0])
        if k % 2 == 0:
            pltpu.make_async_remote_copy(
                left, left, ag_send.at[k, 2], ag_recv.at[k, 2],
                device_id=(z, loc((x + 1) % 4, c), y), device_id_type=MESH,
            ).start()
        to_sib(left, k, 1)
        take(right, ag_recv.at[k, 1])
        if k % 2 == 1:
            pltpu.make_async_remote_copy(
                right, right, ag_send.at[k, 2], ag_recv.at[k, 2],
                device_id=(z, loc((x + 3) % 4, c), y), device_id_type=MESH,
            ).start()
        to_sib(right, k, 2)

    def across(k):
        far = rall.at[(x + 2) % 4, c, k]
        take(far, ag_recv.at[k, 2])
        to_sib(far, k, 3)

    def settle(k):
        for n, dx in enumerate((0, 3, 1, 2)):
            take(rall.at[(x + dx) % 4, oc, k], as_recv.at[k, n])

    def half(h):
        lo = 192 * h
        rows = slice(lo, lo + 192)
        lane192 = iota((192, 128), 1) < 64
        for p in range(4):
            te = rall[p, 0, 4 * h : 4 * h + 4].reshape(192, 640)
            to = rall[p, 1, 4 * h : 4 * h + 4].reshape(192, 640)
            te_t = te[:, 256:384].astype(F32)
            to_t = to[:, 256:384].astype(F32)
            b = p * 640
            xf[rows, b : b + 256] = te[:, 0:256]
            xf[rows, b + 256 : b + 384] = jnp.where(lane192, te_t, to_t).astype(BF)
            xf[rows, b + 384 : b + 640] = to[:, 0:256]
            df[rows, b : b + 256] = te[:, 384:640]
            df[rows, b + 256 : b + 384] = jnp.where(
                lane192, pltpu.roll(te_t, 64, 1), pltpu.roll(to_t, 64, 1)
            ).astype(BF)
            df[rows, b + 384 : b + 640] = to[:, 384:640]
        ab = nt(xf[rows, :], wgu[...])
        e = nt(df[rows, :], ed_ref[0])
        a = ab[:, 0:96]
        b = ab[:, 96:192]
        sg = 1.0 / (1.0 + jnp.exp(-a))
        sl = a * sg
        hid = sl * b
        gpart = jnp.sum(e * hid, axis=1, keepdims=True)
        q = qv[rows, 0:1]
        qe = q * e
        dab[rows, :] = jnp.concatenate([qe * b * sg * (1.0 + a * (1.0 - sg)), qe * sl], axis=1).astype(BF)
        hq[rows, :] = (q * hid).astype(BF)
        rd[...] = nn(dab[rows, :], wgu[...]).astype(BF)
        for k in range(4):
            r48 = slice(k * 48, (k + 1) * 48)
            g = jnp.where(lane48 == c48, gpart[r48], 0.0).astype(BF)
            zero = jnp.zeros((48, 128), F32)
            cols = []
            for p in range(4):
                t = rd[r48, p * 640 + 256 : p * 640 + 384].astype(F32)
                u = pltpu.roll(t, 64, 1)
                for cc in range(2):
                    b = p * 640 + cc * 384
                    first, second = (t, u) if cc == 0 else (u, t)
                    cols.append(
                        jnp.concatenate(
                            [
                                rd[r48, b : b + 128],
                                rd[r48, b + 128 : b + 256],
                                jnp.where(low48, first, zero).astype(BF),
                                jnp.where(low48, zero, second).astype(BF),
                                g,
                            ],
                            axis=0,
                        )
                    )
            packed = nn(qr[...], jnp.concatenate(cols, axis=1)).astype(BF)
            for ll in range(8):
                pkb[h, ll, k] = packed[:, ll * 128 : (ll + 1) * 128]
        for o in (2, 1, 3, 0):
            xx = (x + o) % 4
            pltpu.make_async_remote_copy(
                pkb.at[h, loc(xx, oc)], s1.at[h, xx], c_send.at[h, o], c_recv.at[h, o],
                device_id=(z, loc(x, oc), y), device_id_type=MESH,
            ).start()

    def reduce_pair(h):
        for o in (2, 1, 3, 0):
            xx = (x + o) % 4
            take(s1.at[h, xx], c_recv.at[h, o])
            v = (pkb[h, loc(xx, c)].astype(F32) + s1[h, xx].astype(F32)).astype(BF)
            if o == 0:
                s3[h, x] = v
            else:
                s2[h, xx] = v
                pltpu.make_async_remote_copy(
                    s2.at[h, xx], s3.at[h, x], r_send.at[h, o], r_recv.at[h, o],
                    device_id=(z, loc(xx, c), y), device_id_type=MESH,
                ).start()

    def give_back(h):
        for o in (1, 2, 3):
            take(s3.at[h, (x + 4 - o) % 4], r_recv.at[h, o])
        for k in range(4):
            v = s3[h, 0, k].astype(F32) + s3[h, 1, k].astype(F32)
            v = v + s3[h, 2, k].astype(F32) + s3[h, 3, k].astype(F32)
            ret[h, k] = v.astype(BF).reshape(8, 16, 128)
            kk = 4 * h + k
            for n, dz in enumerate((8 - kk, (8 + kk) % 16 if kk else 0)):
                for j in range(4):
                    src = ret.at[h, k, n * 4 + j]
                    dst = back.at[dz, y]
                    if dz == 0:

                        @pl.when(y == j)
                        def _():
                            pltpu.make_async_copy(src, dst, b_recv).start()

                        @pl.when(y != j)
                        def _():
                            pltpu.make_async_remote_copy(
                                src, dst, b_send, b_recv, device_id=(z, l, j), device_id_type=MESH
                            ).start()

                    else:
                        pltpu.make_async_remote_copy(
                            src, dst, b_send, b_recv,
                            device_id=((z + 16 - dz) % 16, l, j), device_id_type=MESH,
                        ).start()

    def dx_out():
        take(dxs, ds_recv)
        for i in range(4):
            own = jnp.logical_and(x == y, y == i)
            dxf[i] = (dxp[c, i].astype(F32) + dxs[i].astype(F32)).astype(BF)

            @pl.when(own)
            def _():
                pltpu.make_async_copy(dxf.at[i], dxr.at[x], dx_recv.at[x]).start()

            @pl.when(jnp.logical_not(own))
            def _():
                pltpu.make_async_remote_copy(
                    dxf.at[i], dxr.at[x], dx_send.at[i], dx_recv.at[x],
                    device_id=(z, loc(y, c), i), device_id_type=MESH,
                ).start()

    low128 = lane < 64

    def group_in(o):
        i = (y + o) % 4
        take(xs.at[i, c], tok_recv.at[i])
        pltpu.make_async_remote_copy(
            xs.at[i, c], xs.at[i, c], tsib_send.at[i], tsib_recv.at[i],
            device_id=(z, loc(x, oc), y), device_id_type=MESH,
        ).start()

    def group_forward(o):
        i = (y + o) % 4
        take(xs.at[i, oc], tsib_recv.at[i])
        te = xs[i, 0]
        to = xs[i, 1]
        te_t = te[:, 256:384].astype(F32)
        to_t = to[:, 256:384].astype(F32)
        rows = pl.ds(pl.multiple_of(i * 128, 128), 128)
        xa[rows, 0:256] = te[:, 0:256]
        xa[rows, 256:384] = jnp.where(low128, te_t, to_t).astype(BF)
        xa[rows, 384:640] = to[:, 0:256]
        da[rows, 0:256] = te[:, 384:640]
        da[rows, 256:384] = jnp.where(low128, pltpu.roll(te_t, 64, 1), pltpu.roll(to_t, 64, 1)).astype(BF)
        da[rows, 384:640] = to[:, 384:640]
        sp[i, :, 0:384] = nt(xa[rows, :], wsg[...]).astype(BF)
        sp[i, :, 384:576] = nt(da[rows, :], sd_ref[...]).astype(BF)
        sp[i, :, 576:640] = jnp.zeros((128, 64), BF)
        if o:
            pltpu.make_async_remote_copy(
                sp.at[i], r2.at[y], y_send.at[o], y_recv.at[o],
                device_id=(z, l, i), device_id_type=MESH,
            ).start()
        else:
            r2[y] = sp[y]

    group_in(1)
    group_in(3)
    group_forward(1)
    group_in(2)
    group_forward(3)
    group_in(0)
    group_forward(2)
    group_forward(0)
    jc = iota((128, 1024), 1)
    jr = jc & 15
    jg = lax.shift_right_arithmetic(jc, 4) * 6
    cls_a = jr < 6
    cls_b = jnp.logical_and(jr >= 6, jr < 12)
    cls_t = jnp.logical_and(jr >= 12, jr < 15)
    code = jg + jnp.where(cls_a, jr, jnp.where(cls_b, jr - 6, jr - 12))
    pos = jnp.where(rs >= 0, ex * 6 + rs, -100)
    hit = code == pos[:, 0:1]
    hit2 = code + 3 == pos[:, 0:1]
    for kk in range(1, 6):
        hit = jnp.logical_or(hit, code == pos[:, kk : kk + 1])
        hit2 = jnp.logical_or(hit2, code + 3 == pos[:, kk : kk + 1])
    selm[...] = jnp.concatenate(
        [
            one(jnp.logical_and(hit, cls_a)),
            one(jnp.logical_and(hit, cls_b)),
            one(jnp.logical_and(hit, cls_t)),
            one(jnp.logical_and(hit2, cls_t)),
        ],
        axis=0,
    )
    grow = one(jnp.logical_and(iota((64, 1024), 1) == iota((64, 1024), 0) * 16 + 15, True))
    unpack(0)
    unpack(1)
    forward(0)
    unpack(2)
    forward(1)
    across(0)
    unpack(3)
    forward(2)
    across(1)

    for o in range(1, 4):
        take(r2.at[(y + 4 - o) % 4], y_recv.at[o])
    tot = r2[0].astype(F32) + r2[1].astype(F32) + r2[2].astype(F32) + r2[3].astype(F32)
    sa = tot[:, 0:192]
    sb = tot[:, 192:384]
    se = tot[:, 384:576]
    sig = 1.0 / (1.0 + jnp.exp(-sa))
    sil = sa * sig
    sdall[y] = jnp.concatenate(
        [
            se * sb * sig * (1.0 + sa * (1.0 - sig)),
            se * sil,
            sil * sb,
            jnp.zeros((128, 64), F32),
        ],
        axis=1,
    ).astype(BF)
    for o in range(1, 4):
        pltpu.make_async_remote_copy(
            sdall.at[y], sdall.at[y], y2_send.at[o], y2_recv.at[o],
            device_id=(z, l, (y + o) % 4), device_id_type=MESH,
        ).start()
    unpack(4)
    forward(3)
    across(2)
    unpack(5)
    forward(4)
    across(3)

    for o in range(1, 4):
        take(sdall.at[(y + 4 - o) % 4], y2_recv.at[o])
    sall = sdall[...].reshape(512, 640)
    for t in range(5):
        cols = slice(t * 128, (t + 1) * 128)
        g2 = tn(sall[:, 0:384], xa[:, cols])
        g1 = tn(sall[:, 384:640], da[:, cols])
        gp[t * 3] = g2[0:192].astype(BF)
        gp[t * 3 + 1] = g2[192:384].astype(BF)
        gp[t * 3 + 2] = g1[0:192].astype(BF)
    gp[15] = jnp.zeros((192, 128), BF)

    ring(0)
    unpack(6)
    forward(5)
    across(4)
    unpack(7)
    forward(6)
    across(5)
    ring(1)
    for i in range(4):
        part = nn(sall[i * 128 : (i + 1) * 128, 0:384], wsg[...]).astype(BF)
        dxp[0, i] = part[:, 0:384]
        dxp[1, i] = part[:, 256:640]
    pltpu.make_async_remote_copy(
        dxp.at[oc], dxs, ds_send, ds_recv, device_id=(z, loc(x, oc), y), device_id_type=MESH
    ).start()

    for k in range(4):
        settle(k)
    half(0)
    ring(2)
    forward(7)
    across(6)
    across(7)
    reduce_pair(0)
    ring(3)
    for k in range(4, 8):
        settle(k)
    half(1)
    ring(4)
    give_back(0)
    reduce_pair(1)
    dx_out()
    def weight_grads(i, _):
        cols = pl.ds(pl.multiple_of(i * 640, 128), 640)
        g2 = tn(dab[...], xf[:, cols])
        neg_ref[0, :, cols] = g2[0:96].astype(BF)
        neu_ref[0, :, cols] = g2[96:192].astype(BF)
        ned_ref[0, :, cols] = tn(hq[...], df[:, cols]).astype(BF)
        return 0

    lax.fori_loop(0, 2, weight_grads, 0)
    ring(5)
    lax.fori_loop(2, 4, weight_grads, 0)


    give_back(1)
    ring(6)
    ring(7)

    take(back, b_recv)
    rows = back[...].reshape(1024, 128)
    got = nn(selm[...], rows)
    gates = nn(grow, rows).astype(BF)
    lane64 = iota((128, 64), 1)
    acc = jnp.zeros((128, 128), F32)
    for kk in range(6):
        gk = nn(one(lane64 == ex[:, kk : kk + 1]), gates)
        gk = jnp.sum(jnp.where(lane == rs[:, kk : kk + 1], gk, 0.0), axis=1, keepdims=True)
        acc = jnp.where(lane == kk, gk, acc)
    gg_ref[...] = acc.T[0:6, :]
    for i in range(4):
        take(dxr.at[i], dx_recv.at[i])
    m = dxr[0].astype(F32) + dxr[1].astype(F32) + dxr[2].astype(F32) + dxr[3].astype(F32)
    tl = got[256:384, 0:64] + got[384:512, 64:128]
    evn = jnp.concatenate([m[:, 0:128] + got[0:128], m[:, 128:256] + got[128:256], m[:, 256:320] + tl], axis=1)
    od = jnp.concatenate([m[:, 64:128] + tl, m[:, 128:256] + got[0:128], m[:, 256:384] + got[128:256]], axis=1)
    gx_ref[...] = tn(jnp.where(is_even, evn, od).astype(BF), eye).astype(BF)

    ring(8)
    for t in range(5):
        cols = slice(t * 128, (t + 1) * 128)
        gsg_ref[:, cols] = fo[t * 3]
        gsu_ref[:, cols] = fo[t * 3 + 1]
        gsd_ref[:, cols] = fo[t * 3 + 2]

    for i in range(4):
        own = jnp.logical_and(x == i, y == x)

        @pl.when(jnp.logical_not(own))
        def _():
            take(tx, tok_send.at[i])

        take(xs.at[i, c], tsib_send.at[i])
        own2 = jnp.logical_and(x == y, y == i)

        @pl.when(jnp.logical_not(own2))
        def _():
            take(dxf.at[i], dx_send.at[i])

    pbf = pb.reshape(64, 32, 128)
    take(pbf.at[0:63], disp_send)
    backf = back.reshape(64, 16, 128)
    take(backf.at[0:63], b_send)
    for o in range(1, 4):
        take(sp.at[0], y_send.at[o])
        take(sdall.at[0], y2_send.at[o])
    take(dxs, ds_send)
    for k in range(8):
        for n in range(3):
            take(rall.at[0, 0, k], ag_send.at[k, n])
        for n in range(4):
            take(rall.at[0, 0, k], as_send.at[k, n])
    for h in range(2):
        for o in range(4):
            take(s1.at[h, 0], c_send.at[h, o])
        for o in range(1, 4):
            take(s2.at[h, 0], r_send.at[h, o])
    for u in range(2):
        w = pl.ds(u * 96, 96)
        for q in range(4):
            take(fo.at[0, w], ra_send.at[q, u])
            take(fo.at[0, w], ro_send.at[q, u])
            take(fo.at[0, w], lo_send.at[q, u])
            take(fo.at[0, w], be_send.at[q, u])
            take(fo.at[0, w], bo_send.at[q, u])
            take(fo.at[0, w], ll_send.at[q, u])
        for q in range(3):
            take(fo.at[0, w], la_send.at[q, u])
            take(fo.at[0, w], le_send.at[q, u])


def hand_over(*refs):
    held, came, left = refs[16:24], refs[24], refs[25]
    inward = [pltpu.make_async_copy(refs[i], held[i], came.at[i]) for i in range(8)]
    outward = [pltpu.make_async_copy(held[i], refs[8 + i], left.at[i]) for i in range(8)]
    for copy in inward:
        copy.start()
    for i in range(8):
        inward[i].wait()
        outward[i].start()
    for copy in outward:
        copy.wait()


def on_device(*args):
    sem = pltpu.SemaphoreType.DMA
    vm = pltpu.VMEM
    out_shape = (
        jax.ShapeDtypeStruct((320, 128), BF),
        jax.ShapeDtypeStruct((6, 128), F32),
        jax.ShapeDtypeStruct((192, 640), BF),
        jax.ShapeDtypeStruct((192, 640), BF),
        jax.ShapeDtypeStruct((192, 640), BF),
        jax.ShapeDtypeStruct((1, 96, 2560), BF),
        jax.ShapeDtypeStruct((1, 96, 2560), BF),
        jax.ShapeDtypeStruct((1, 96, 2560), BF),
    )
    scratch = [
        vm((128, 640), BF),
        vm((16, 4, 32, 128), BF),
        vm((16, 4, 32, 128), BF),
        vm((768, 128), BF),
        vm((288, 256), BF),
        vm((128, 240), BF),
        vm((4, 2, 8, 48, 640), BF),
        vm((384, 128), F32),
        vm((384, 2560), BF),
        vm((384, 2560), BF),
        vm((192, 2560), BF),
        vm((384, 192), BF),
        vm((384, 96), BF),
        vm((2, 8, 4, 128, 128), BF),
        vm((2, 4, 4, 128, 128), BF),
        vm((2, 4, 4, 128, 128), BF),
        vm((2, 4, 4, 128, 128), BF),
        vm((2, 4, 8, 16, 128), BF),
        vm((16, 4, 16, 128), BF),
        vm((192, 2560), BF),
        vm((4, 2, 128, 640), BF),
        vm((512, 640), BF),
        vm((512, 640), BF),
        vm((384, 640), BF),
        vm((4, 128, 640), BF),
        vm((4, 128, 640), BF),
        vm((4, 128, 640), BF),
        vm((2, 4, 128, 384), BF),
        vm((4, 128, 384), BF),
        vm((4, 128, 384), BF),
        vm((4, 128, 384), BF),
        vm((16, 192, 128), BF),
        vm((4, 192, 128), BF),
        vm((4, 192, 128), BF),
        vm((3, 192, 128), BF),
        vm((4, 192, 128), BF),
        vm((16, 192, 128), BF),
        vm((512, 1024), BF),
        sem((4,)), sem((4,)), sem((4,)), sem((4,)), sem, sem((8,)),
        sem((8, 3)), sem((8, 3)), sem((8, 4)), sem((8, 4)),
        sem((4,)), sem((4,)), sem((4,)), sem((4,)),
        sem, sem, sem((4,)), sem((4,)),
        sem((4, 2)), sem((4, 2)), sem((4, 2)), sem((4, 2)),
        sem((3, 2)), sem((3, 2)), sem((4, 2)), sem((4, 2)),
        sem((4, 2)), sem((4, 2)), sem((4, 2)), sem((4, 2)),
        sem((3, 2)), sem((3, 2)), sem((4, 2)), sem((4, 2)),
        sem((2, 4)), sem((2, 4)), sem((2, 4)), sem((2, 4)), sem, sem,
    ]
    x, dy, gv, re, rs = [v.T for v in args[:5]]
    outs = pl.pallas_call(
        kernel,
        out_shape=out_shape,
        in_specs=[pl.BlockSpec(memory_space=pltpu.VMEM)] * 11,
        out_specs=tuple([pl.BlockSpec(memory_space=pltpu.VMEM)] * 8),
        scratch_shapes=scratch,
        compiler_params=pltpu.CompilerParams(
            collective_id=0, has_side_effects=True, vmem_limit_bytes=56 * 1024 * 1024
        ),
        cost_estimate=pl.CostEstimate(flops=3_000_000_000, bytes_accessed=6_000_000, transcendentals=100_000),
    )(x, dy, gv, re, rs, *args[5:])
    outs = pl.pallas_call(
        hand_over,
        out_shape=out_shape,
        in_specs=[pl.BlockSpec(memory_space=pl.ANY)] * 8,
        out_specs=tuple([pl.BlockSpec(memory_space=pl.ANY)] * 8),
        scratch_shapes=[vm(v.shape, v.dtype) for v in out_shape] + [sem((8,)), sem((8,))],
        compiler_params=pltpu.CompilerParams(vmem_limit_bytes=60 * 1024 * 1024),
        cost_estimate=pl.CostEstimate(flops=0, bytes_accessed=5_000_000, transcendentals=0),
    )(*outs)
    return (outs[0].T, outs[1].T, *outs[2:])


def solution(mesh):
    in_specs = (
        P(("node", "dp"), "local"),
        P(("node", "dp"), "local"),
        P(("node", "dp"), None),
        P(("node", "dp"), None),
        P(("node", "dp"), None),
        P("local", "dp"),
        P("local", "dp"),
        P("local", "dp"),
        P(("node", "dp"), "local", None),
        P(("node", "dp"), "local", None),
        P(("node", "dp"), "local", None),
    )
    out_specs = (
        P(("node", "dp"), "local"),
        P(("node", "dp"), None),
        P("local", "dp"),
        P("local", "dp"),
        P("local", "dp"),
        P(("node", "dp"), "local", None),
        P(("node", "dp"), "local", None),
        P(("node", "dp"), "local", None),
    )
    return jax.shard_map(
        on_device, mesh=mesh, in_specs=in_specs, out_specs=out_specs, check_vma=False
    )
```
